256 devices in a mesh: dp: 32 (over z, y_lo, core), orient: 8 (over x, y_hi).
Axes of the slice: x: 4, y: 4 (y_hi: 2, y_lo: 2; y = y_hi * 2 + y_lo), z: 8, core: 2. Of those that a mesh axis runs over, the one named last changes fastest.
Arguments:
- images: bfloat16 [16384, 8448], P(('dp', 'orient')), may hold values from -180 to 180
- groups: int32 [16384], P(('dp', 'orient')), may hold values from 0 to 63, as said below
- panel_slots: bfloat16 [32, 512, 8448], P('dp', 'orient'), may hold values from -0.12 to 0.12
- owners: int32 [8], replicated, may hold values from 0 to 31, as said below
- contrast: float32 [64, 4224], replicated, may hold values from -1 to 1
- noise_weight: float32 [4224], replicated, may hold values from 0.5 to 4
- class_prior: float32 [8], replicated, may hold values from -1.5 to 0
Outputs:
- log_evidence: float32 [16384], P(('dp', 'orient'))
- class_posterior: float32 [8, 16384], P(None, ('dp', 'orient'))
- orientation_mass: float32 [8, 512], P(None, 'orient')
The draws below stay inside these ranges and needn't reach their ends.
Inputs may be any that keep to these rules, and one draw needn't show every extreme that they name: `owners`: distinct; the largest index 31 owns some class. `groups`: group 64 - 1 holds some particle.
All inputs are finite; a program needn't handle non-finite values.
Results may differ from the reference program's by a relative error of at most 0.0021.
Values may be sent and summed in bfloat16 or wider, within the bound.
No kernel may reach another device: no remote copies, remote signals or barrier semaphores. Data moves between devices by JAX's collectives and lax.ppermute only.
A program may use at most 128 MiB of HBM per device.

```python
import math
import jax
import jax.numpy as jnp
from jax import lax

CLASSES = 8
PIXELS = 4224
GROUPS = 64
FEATURES = 8448
ORIENTS = 512
PARTICLES = 16384
N_DP = 32


def shared_parts(key):
    owner_key = jax.random.fold_in(key, 101)
    order_key = jax.random.fold_in(key, 102)
    group_key = jax.random.fold_in(key, 103)
    radius_key = jax.random.fold_in(key, 104)
    focus_key = jax.random.fold_in(key, 105)
    bfactor_key = jax.random.fold_in(key, 106)
    noise_key = jax.random.fold_in(key, 107)
    panel_key = jax.random.fold_in(key, 108)
    chosen = jax.random.permutation(owner_key, N_DP - 1)[:CLASSES - 1].astype(jnp.int32)
    listed = jnp.concatenate([chosen, jnp.full((1,), N_DP - 1, jnp.int32)])
    owners = listed[jax.random.permutation(order_key, CLASSES)].astype(jnp.int32)
    groups = jax.random.randint(group_key, (PARTICLES,), 0, GROUPS).astype(jnp.int32)
    groups = groups.at[0].set(GROUPS - 1)
    radius = jax.random.uniform(radius_key, (1, PIXELS), jnp.float32, 0.02, 0.5)
    focus = jnp.exp(jax.random.uniform(focus_key, (GROUPS, 1), jnp.float32, math.log(60.0), math.log(400.0)))
    bfactor = jax.random.uniform(bfactor_key, (GROUPS, 1), jnp.float32, 2.0, 8.0)
    contrast = -jnp.sin(focus * radius * radius + 0.1) * jnp.exp(-bfactor * radius * radius)
    noise_weight = jnp.exp(jax.random.uniform(noise_key, (PIXELS,), jnp.float32, math.log(0.5), math.log(4.0)))
    base = jax.random.normal(panel_key, (N_DP, ORIENTS, FEATURES), jnp.float32) / math.sqrt(FEATURES)
    panels = jnp.clip(base, -0.119, 0.119)
    return (owners, groups, contrast, noise_weight, panels)


def draw_owners(key, part):
    owners, groups, contrast, noise_weight, panels = shared_parts(key)
    return owners


def draw_groups(key, part):
    owners, groups, contrast, noise_weight, panels = shared_parts(key)
    return groups


def draw_contrast(key, part):
    owners, groups, contrast, noise_weight, panels = shared_parts(key)
    return contrast


def draw_noise_weight(key, part):
    owners, groups, contrast, noise_weight, panels = shared_parts(key)
    return noise_weight


def draw_panel_slots(key, part):
    owners, groups, contrast, noise_weight, panels = shared_parts(key)
    return panels.astype(jnp.bfloat16)


def draw_images(key, part):
    key = jax.random.fold_in(key, 12)
    values = jnp.clip(1.5 * jax.random.normal(key, (PARTICLES, FEATURES), jnp.float32), -8.0, 8.0)
    return values.astype(jnp.bfloat16)


def setup_inputs(seed: int = 0) -> dict:
    key_of = jax.random.split(jax.random.key(seed), 8)
    images = draw_images(jax.random.fold_in(key_of[7], 71), 0)
    groups = draw_groups(jax.random.fold_in(key_of[7], 71), 0)
    panel_slots = draw_panel_slots(jax.random.fold_in(key_of[7], 71), 0)
    owners = draw_owners(jax.random.fold_in(key_of[7], 71), 0)
    contrast = draw_contrast(jax.random.fold_in(key_of[7], 71), 0)
    noise_weight = draw_noise_weight(jax.random.fold_in(key_of[7], 71), 0)
    class_prior = jnp.clip(jax.random.uniform(key_of[6], (CLASSES,), jnp.float32, -1.5, 0.0), -1.5, 0.0)
    return dict(images=images, groups=groups, panel_slots=panel_slots, owners=owners, contrast=contrast, noise_weight=noise_weight, class_prior=class_prior)


def reference(images, groups, panel_slots, owners, contrast, noise_weight, class_prior):
    hot_groups = (groups[:, None] == jnp.arange(GROUPS, dtype=jnp.int32)[None, :]).astype(jnp.float32)
    row_contrast = jnp.dot(hot_groups, contrast, precision=lax.Precision.HIGHEST)
    factor = row_contrast * noise_weight[None, :]
    weighted = (images.astype(jnp.float32) * jnp.concatenate([factor, factor], axis=1)).astype(jnp.bfloat16)
    power = contrast * contrast * noise_weight[None, :]

    def one_class(class_id):
        panel = panel_slots[owners[class_id]]
        squared = panel.astype(jnp.float32) ** 2
        power_sum = squared[:, :PIXELS] + squared[:, PIXELS:]
        table = lax.dot_general(power, power_sum, (((1,), (1,)), ((), ())), precision=lax.Precision.HIGHEST)
        crossed = lax.dot_general(panel, weighted, (((1,), (1,)), ((), ())), preferred_element_type=jnp.float32)
        penalty = lax.dot_general(table, hot_groups, (((0,), (1,)), ((), ())), precision=lax.Precision.HIGHEST)
        return crossed - 0.5 * penalty + class_prior[class_id]

    scores = lax.map(one_class, jnp.arange(CLASSES, dtype=jnp.int32))
    maximum = jnp.max(scores, axis=1)
    class_lse = maximum + jnp.log(jnp.sum(jnp.exp(scores - maximum[:, None, :]), axis=1))
    top = jnp.max(class_lse, axis=0)
    log_evidence = top + jnp.log(jnp.sum(jnp.exp(class_lse - top[None, :]), axis=0))
    class_posterior = jnp.exp(class_lse - log_evidence[None, :])
    normalise = CLASSES * ORIENTS / PARTICLES
    orientation_mass = jnp.sum(jnp.exp(scores - log_evidence[None, None, :]), axis=2) * normalise
    return log_evidence, class_posterior, orientation_mass
```

```python
import functools
import jax
import jax.numpy as jnp
from jax import lax
from jax.experimental import pallas as pl
from jax.experimental.pallas import tpu as pltpu
from jax.sharding import PartitionSpec as P

NZ, NYLO, NCORE = 8, 2, 2
NDP, NOR = 32, 8
CLS, PIX, GRP, ORI, ROWS = 8, 4224, 64, 64, 64
FEAT = 2 * PIX
EXT = 256
COLS = FEAT + EXT
HALF = COLS // 2
QUART = COLS // 4
GROUP_ROWS = NOR * ROWS
HIGH = lax.Precision.HIGHEST
NT = (((1,), (1,)), ((), ()))
MIB = 1024 * 1024


def permute(array, move):
    pairs = []
    for dp in range(NDP):
        z, ylo, core = dp // 4, (dp // 2) % 2, dp % 2
        nz, nylo, ncore = move(z, ylo, core)
        target = (nz % NZ) * 4 + nylo * 2 + ncore
        for orient in range(NOR):
            pairs.append((dp * NOR + orient, target * NOR + orient))
    return lax.ppermute(array, ("dp", "orient"), pairs)


def other_core(array):
    return permute(array, lambda z, ylo, core: (z, ylo, 1 - core))


def other_ylo(array):
    return permute(array, lambda z, ylo, core: (z, 1 - ylo, core))


def from_below(array):
    return permute(array, lambda z, ylo, core: (z + 1, ylo, core))


def from_above(array):
    return permute(array, lambda z, ylo, core: (z - 1, ylo, core))


def vmem():
    return pl.BlockSpec(memory_space=pltpu.VMEM)


def smem():
    return pl.BlockSpec(memory_space=pltpu.SMEM)


def params(mib, **more):
    return pltpu.CompilerParams(vmem_limit_bytes=mib * MIB, **more)


def weigh_kernel(core_ref, images_ref, groups_ref, contrast_ref, noise_ref, out_ref):
    core = core_ref[0]
    hot = (
        groups_ref[...] == lax.broadcasted_iota(jnp.int32, (ROWS, GRP), 1)
    ).astype(jnp.float32)
    rows = jnp.dot(hot, contrast_ref[...], precision=HIGH, preferred_element_type=jnp.float32)
    factor = rows * noise_ref[...]
    real = (images_ref[:, :PIX].astype(jnp.float32) * factor).astype(jnp.bfloat16)
    imag = (images_ref[:, PIX:].astype(jnp.float32) * factor).astype(jnp.bfloat16)
    out_ref[core, :, :PIX] = real
    out_ref[core, :, PIX:] = imag[:, : HALF - PIX]
    out_ref[1 - core, :, : FEAT - HALF] = imag[:, HALF - PIX :]
    ext = jnp.concatenate([hot, hot, hot, jnp.zeros_like(hot)], axis=1)
    out_ref[1 - core, :, FEAT - HALF :] = ext.astype(jnp.bfloat16)


def weigh(core, images, groups, contrast, noise):
    return pl.pallas_call(
        weigh_kernel,
        out_shape=jax.ShapeDtypeStruct((2, ROWS, HALF), jnp.bfloat16),
        in_specs=[smem(), vmem(), vmem(), vmem(), vmem()],
        out_specs=vmem(),
        compiler_params=params(24),
        name="weigh",
    )(core, images, groups, contrast, noise)


def panel_kernel(prior_ref, slot_ref, contrast_ref, noise_ref, out_ref):
    contrast = contrast_ref[...]
    power = contrast * contrast * noise_ref[...]
    real = slot_ref[:, :PIX].astype(jnp.float32)
    imag = slot_ref[:, PIX:].astype(jnp.float32)
    table = lax.dot_general(
        real * real + imag * imag, power, NT, precision=HIGH, preferred_element_type=jnp.float32
    )
    table = -0.5 * table + prior_ref[0]
    first = table.astype(jnp.bfloat16).astype(jnp.float32)
    rest = table - first
    second = rest.astype(jnp.bfloat16).astype(jnp.float32)
    third = rest - second
    ext = jnp.concatenate([first, second, third, jnp.zeros_like(first)], axis=1)
    for z in range(NZ):
        rows = slice(8 * z, 8 * z + 8)
        for ylo in range(NYLO):
            parts = []
            for core in range(NCORE):
                start = core * HALF + ylo * QUART
                stop = start + QUART
                if stop <= FEAT:
                    part = slot_ref[:, start:stop].astype(jnp.float32)[rows]
                else:
                    part = jnp.concatenate(
                        [slot_ref[:, start:FEAT].astype(jnp.float32)[rows], ext[rows]], axis=1
                    )
                parts.append(part)
            at = (z * 4 + ylo * 2) * 8
            out_ref[at : at + 16, :] = jnp.concatenate(parts, axis=0).astype(jnp.bfloat16)


def panel(prior, slot, contrast, noise):
    return pl.pallas_call(
        panel_kernel,
        out_shape=jax.ShapeDtypeStruct((NDP * 8, QUART), jnp.bfloat16),
        in_specs=[smem(), vmem(), vmem(), vmem()],
        out_specs=vmem(),
        compiler_params=params(24),
        name="panel",
    )(prior, slot, contrast, noise)


def scores_kernel(panel_ref, images_ref, out_ref):
    part = lax.dot_general(
        panel_ref[...].reshape(NZ * CLS * 8, QUART),
        images_ref[...].reshape(GROUP_ROWS, QUART),
        NT,
        preferred_element_type=jnp.float32,
    )

    @pl.when(pl.program_id(0) == 0)
    def _():
        out_ref[...] = part

    @pl.when(pl.program_id(0) != 0)
    def _():
        out_ref[...] += part


def scores_of(panels, images, which):
    rows = NZ * CLS * 8
    return pl.pallas_call(
        scores_kernel,
        grid=(NYLO,),
        out_shape=jax.ShapeDtypeStruct((rows, GROUP_ROWS), jnp.float32),
        in_specs=[
            pl.BlockSpec((NZ, 1, CLS * 8, QUART), lambda y: (0, y, 0, 0)),
            pl.BlockSpec((NOR, 1, ROWS, QUART), lambda y: (0, which, 0, y)),
        ],
        out_specs=pl.BlockSpec((rows, GROUP_ROWS), lambda y: (0, 0)),
        compiler_params=params(32),
        cost_estimate=pl.CostEstimate(
            flops=2 * rows * GROUP_ROWS * HALF, bytes_accessed=10 * MIB, transcendentals=0
        ),
        name="scores",
    )(panels, images)


def norms_kernel(mine_ref, other_ref, scores_ref, lse_ref):
    scores = mine_ref[...] + other_ref[...]
    scores_ref[...] = scores
    scores = scores.reshape(NZ, CLS, 8, GROUP_ROWS)
    maximum = jnp.max(jnp.max(scores, axis=0), axis=1, keepdims=True)
    totals = jnp.sum(jnp.sum(jnp.exp(scores - maximum[None]), axis=0), axis=1)
    lse_ref[...] = maximum[:, 0, :] + jnp.log(totals)


def norms(mine, other):
    return pl.pallas_call(
        norms_kernel,
        out_shape=(
            jax.ShapeDtypeStruct(mine.shape, jnp.float32),
            jax.ShapeDtypeStruct((CLS, GROUP_ROWS), jnp.float32),
        ),
        in_specs=[vmem(), vmem()],
        out_specs=(vmem(), vmem()),
        compiler_params=params(24),
        name="norms",
    )(mine, other)


def finish_kernel(shift_ref, parts_ref, scores_ref, evidence_ref, posterior_ref, mass_ref):
    parts = parts_ref[...]
    maximum = jnp.max(parts, axis=0)
    class_lse = maximum + jnp.log(jnp.sum(jnp.exp(parts - maximum[None]), axis=0))
    top = jnp.max(class_lse, axis=0, keepdims=True)
    evidence = top + jnp.log(jnp.sum(jnp.exp(class_lse - top), axis=0, keepdims=True))
    evidence_ref[...] = evidence
    posterior_ref[...] = jnp.exp(class_lse - evidence)
    terms = jnp.exp(scores_ref[...] - evidence)
    ones = jnp.ones((8, GROUP_ROWS), jnp.float32)
    mass = lax.dot_general(ones, terms, NT, precision=HIGH, preferred_element_type=jnp.float32)
    mass_ref[...] = pltpu.roll(mass, shift_ref[0], 1)


def finish(shift, parts, scores):
    return pl.pallas_call(
        finish_kernel,
        out_shape=(
            jax.ShapeDtypeStruct((1, GROUP_ROWS), jnp.float32),
            jax.ShapeDtypeStruct((CLS, GROUP_ROWS), jnp.float32),
            jax.ShapeDtypeStruct((8, scores.shape[0]), jnp.float32),
        ),
        in_specs=[smem(), vmem(), vmem()],
        out_specs=(vmem(), vmem(), vmem()),
        compiler_params=params(24),
        name="finish",
    )(shift, parts, scores)


def per_device(images, groups, panel_slots, owners, contrast, noise_weight, class_prior):
    dp = lax.axis_index("dp")
    orient = lax.axis_index("orient")
    core = dp % 2
    ylo = (dp // 2) % 2
    z = dp // 4
    noise = noise_weight.reshape(1, PIX)
    weighted = weigh(core.reshape(1), images, groups.reshape(ROWS, 1), contrast, noise)
    group = jnp.concatenate([weighted[0], other_core(weighted[1])], axis=0)
    whole = lax.all_gather(group, "orient", axis=0).reshape(NOR, 2, ROWS, HALF)

    prior = jnp.sum(jnp.where(owners == dp, class_prior, 0.0)).reshape(1)
    sent = panel(prior, panel_slots[0], contrast, noise).reshape(NDP, 8, QUART)
    got = lax.all_to_all(sent, "dp", 0, 0)
    mine = jnp.concatenate(
        [lax.dynamic_slice_in_dim(got, owners[k], 1, 0) for k in range(CLS)], axis=0
    )
    theirs = other_ylo(mine)
    first = jnp.where(ylo == 0, mine, theirs)
    second = jnp.where(ylo == 0, theirs, mine)
    block = jnp.stack([first, second]).reshape(NYLO, CLS * 8, QUART)
    up = down = block
    blocks = {0: block}
    for step in (1, 2, 3):
        up, down = from_below(up), from_above(down)
        blocks[NZ - step], blocks[step] = up, down
    blocks[NZ // 2] = jnp.concatenate([from_below(up[:1]), from_above(down[1:])], axis=0)
    panels = jnp.stack([blocks[k] for k in range(NZ)])

    received = other_core(scores_of(panels, whole, 1))
    scores, partial = norms(scores_of(panels, whole, 0), received)
    parts = lax.all_to_all(
        jnp.broadcast_to(partial[None], (NOR, CLS, GROUP_ROWS)), "orient", 0, 0
    )
    evidence, posterior, mass = finish((z * (CLS * 8)).reshape(1), parts, scores)
    masses = lax.all_to_all(jnp.broadcast_to(mass[:1], (NDP, NZ * CLS * 8)), "dp", 0, 0)
    normalise = CLS * ORI * NOR / (ROWS * NOR * NDP)
    total = jnp.sum(masses, axis=0) * normalise
    orientation_mass = total.reshape(NZ, CLS, 8).transpose(1, 0, 2).reshape(CLS, ORI)
    log_evidence = lax.dynamic_slice_in_dim(evidence[0], orient * ROWS, ROWS, 0)
    class_posterior = lax.dynamic_slice_in_dim(posterior, orient * ROWS, ROWS, 1)
    return (log_evidence, class_posterior, orientation_mass)


def solution(mesh):
    return jax.shard_map(
        per_device,
        mesh=mesh,
        in_specs=(
            P(("dp", "orient"), None),
            P(("dp", "orient")),
            P("dp", "orient", None),
            P(),
            P(),
            P(),
            P(),
        ),
        out_specs=(P(("dp", "orient")), P(None, ("dp", "orient")), P(None, "orient")),
        check_vma=False,
    )
```

```python
import functools
import jax
import jax.numpy as jnp
from jax import lax
from jax.experimental import pallas as pl
from jax.experimental.pallas import tpu as pltpu
from jax.sharding import PartitionSpec as P

NX, NZ = 4, 8
NDP, NOR = 32, 8
CLS, PIX, GRP, ORI, ROWS = 8, 4224, 64, 64, 64
FEAT = 2 * PIX
EXT = 256
COLS = FEAT + EXT
HALF = COLS // 2
QUART = COLS // 4
GROUP_ROWS = NOR * ROWS
HIGH = lax.Precision.HIGHEST
NT = (((1,), (1,)), ((), ()))
MIB = 1024 * 1024


def permute(array, move):
    pairs = []
    for dp in range(NDP):
        for orient in range(NOR):
            place = (dp // 4, (dp // 2) % 2, dp % 2, orient // 2, orient % 2)
            z, ylo, core, x, yhi = move(*place)
            target = ((z % NZ) * 4 + ylo * 2 + core) * NOR + (x % NX) * 2 + yhi
            pairs.append((dp * NOR + orient, target))
    return lax.ppermute(array, ("dp", "orient"), pairs)


def other_core(array):
    return permute(array, lambda z, ylo, core, x, yhi: (z, ylo, 1 - core, x, yhi))


def other_ylo(array):
    return permute(array, lambda z, ylo, core, x, yhi: (z, 1 - ylo, core, x, yhi))


def other_yhi(array):
    return permute(array, lambda z, ylo, core, x, yhi: (z, ylo, core, x, 1 - yhi))


def from_below(array):
    return permute(array, lambda z, ylo, core, x, yhi: (z + 1, ylo, core, x, yhi))


def from_above(array):
    return permute(array, lambda z, ylo, core, x, yhi: (z - 1, ylo, core, x, yhi))


def from_left(array):
    return permute(array, lambda z, ylo, core, x, yhi: (z, ylo, core, x + 1, yhi))


def from_right(array):
    return permute(array, lambda z, ylo, core, x, yhi: (z, ylo, core, x - 1, yhi))


def vmem():
    return pl.BlockSpec(memory_space=pltpu.VMEM)


def anywhere():
    return pl.BlockSpec(memory_space=pl.ANY)


def smem():
    return pl.BlockSpec(memory_space=pltpu.SMEM)


def params(mib, **more):
    return pltpu.CompilerParams(vmem_limit_bytes=mib * MIB, **more)


def place():
    dp, orient = lax.axis_index("dp"), lax.axis_index("orient")
    return dp // 4, (dp // 2) % 2, dp % 2, orient // 2, orient % 2


def weigh_kernel(images_ref, groups_ref, contrast_ref, noise_ref, out_ref):
    _, ylo, core, _, _ = place()
    hot = (
        groups_ref[...] == lax.broadcasted_iota(jnp.int32, (ROWS, GRP), 1)
    ).astype(jnp.float32)
    rows = jnp.dot(hot, contrast_ref[...], precision=HIGH, preferred_element_type=jnp.float32)
    factor = rows * noise_ref[...]
    real = (images_ref[:, :PIX].astype(jnp.float32) * factor).astype(jnp.bfloat16)
    imag = (images_ref[:, PIX:].astype(jnp.float32) * factor).astype(jnp.bfloat16)
    ext = jnp.concatenate([hot, hot, hot, jnp.zeros_like(hot)], axis=1).astype(jnp.bfloat16)
    out_ref[core, ylo] = real[:, :QUART]
    out_ref[core, 1 - ylo] = jnp.concatenate([real[:, QUART:], imag[:, : HALF - PIX]], axis=1)
    out_ref[1 - core, ylo] = imag[:, HALF - PIX : 3 * QUART - PIX]
    out_ref[1 - core, 1 - ylo] = jnp.concatenate([imag[:, 3 * QUART - PIX :], ext], axis=1)


def weigh(images, groups, contrast, noise):
    return pl.pallas_call(
        weigh_kernel,
        out_shape=jax.ShapeDtypeStruct((2, 2, ROWS, QUART), jnp.bfloat16),
        in_specs=[vmem(), vmem(), vmem(), vmem()],
        out_specs=vmem(),
        compiler_params=params(24),
        name="weigh",
    )(images, groups, contrast, noise)


def panel_kernel(owners_ref, priors_ref, slot_ref, contrast_ref, noise_ref, out_ref):
    dp = lax.axis_index("dp")
    prior = jnp.float32(0)
    for k in range(CLS):
        prior += jnp.where(owners_ref[k] == dp, priors_ref[k], jnp.float32(0))
    contrast = contrast_ref[...]
    power = contrast * contrast * noise_ref[...]
    real = slot_ref[:, :PIX].astype(jnp.float32)
    imag = slot_ref[:, PIX:].astype(jnp.float32)
    table = lax.dot_general(
        real * real + imag * imag, power, NT, precision=HIGH, preferred_element_type=jnp.float32
    )
    table = -0.5 * table + prior
    first = table.astype(jnp.bfloat16).astype(jnp.float32)
    rest = table - first
    second = rest.astype(jnp.bfloat16).astype(jnp.float32)
    third = rest - second
    ext = jnp.concatenate([first, second, third, jnp.zeros_like(first)], axis=1)
    for z in range(NZ):
        rows = slice(8 * z, 8 * z + 8)
        for ylo in range(2):
            parts = []
            for core in range(2):
                start = core * HALF + ylo * QUART
                stop = start + QUART
                if stop <= FEAT:
                    part = slot_ref[:, start:stop].astype(jnp.float32)[rows]
                else:
                    part = jnp.concatenate(
                        [slot_ref[:, start:FEAT].astype(jnp.float32)[rows], ext[rows]], axis=1
                    )
                parts.append(part)
            at = (z * 4 + ylo * 2) * 8
            out_ref[at : at + 16, :] = jnp.concatenate(parts, axis=0).astype(jnp.bfloat16)


def panel(owners, priors, slot, contrast, noise):
    return pl.pallas_call(
        panel_kernel,
        out_shape=jax.ShapeDtypeStruct((NDP * 8, QUART), jnp.bfloat16),
        in_specs=[smem(), smem(), vmem(), vmem(), vmem()],
        out_specs=vmem(),
        compiler_params=params(24),
        name="panel",
    )(owners, priors, slot, contrast, noise)


def pick_kernel(owners_ref, got_ref, out_ref, sems):
    copies = [
        pltpu.make_async_copy(got_ref.at[owners_ref[k]], out_ref.at[k], sems.at[k])
        for k in range(CLS)
    ]
    for copy in copies:
        copy.start()
    for copy in copies:
        copy.wait()


def pick(owners, got):
    return pl.pallas_call(
        pick_kernel,
        out_shape=jax.ShapeDtypeStruct((CLS, 8, QUART), jnp.bfloat16),
        in_specs=[smem(), anywhere()],
        out_specs=vmem(),
        scratch_shapes=[pltpu.SemaphoreType.DMA((CLS,))],
        compiler_params=params(16),
        name="pick",
    )(owners, got)


def scores_kernel(owners, n_panels, n_images, *refs):
    panels, refs = refs[:n_panels], refs[n_panels:]
    images, refs = refs[:n_images], refs[n_images:]
    outs, (panel_buf, image_buf, panel_sems, image_sems) = refs[: len(owners)], refs[len(owners) :]

    def panel_copies(chain):
        at = 0
        for ref in panels:
            if ref.shape[0] == 1:
                source = ref.at[0] if ref is panels[n_panels - 2 + chain] else None
            else:
                source = ref.at[chain]
            if source is not None:
                target = panel_buf.at[chain, CLS * 8 * at : CLS * 8 * (at + 1)]
                yield pltpu.make_async_copy(source, target, panel_sems.at[chain, at])
                at += 1

    def image_copies(owner, slot, chain):
        for at, ref in enumerate(images):
            target = image_buf.at[slot, chain, ROWS * at : ROWS * (at + 1)]
            yield pltpu.make_async_copy(
                ref.at[owner, chain], target, image_sems.at[slot, chain, at]
            )

    def all_copies(slot, chain):
        copies = list(image_copies(owners[slot], slot, chain))
        return (list(panel_copies(chain)) if slot == 0 else []) + copies

    order = [(slot, chain) for slot in range(len(owners)) for chain in range(2)]
    for slot, chain in order:
        for copy in all_copies(slot, chain):
            copy.start()
    for slot, chain in order:
        for copy in all_copies(slot, chain):
            copy.wait()
        part = lax.dot_general(
            panel_buf[chain], image_buf[slot, chain], NT, preferred_element_type=jnp.float32
        )
        if chain == 0:
            outs[slot][...] = part
        else:
            outs[slot][...] += part


def scores_of(panels, images, owners, blocks):
    rows = blocks * CLS * 8
    outs = len(owners)
    return pl.pallas_call(
        functools.partial(scores_kernel, owners, len(panels), len(images)),
        out_shape=[jax.ShapeDtypeStruct((rows, GROUP_ROWS), jnp.float32)] * outs,
        in_specs=[anywhere()] * (len(panels) + len(images)),
        out_specs=[vmem()] * outs,
        scratch_shapes=[
            pltpu.VMEM((2, rows, QUART), jnp.bfloat16),
            pltpu.VMEM((outs, 2, GROUP_ROWS, QUART), jnp.bfloat16),
            pltpu.SemaphoreType.DMA((2, blocks)),
            pltpu.SemaphoreType.DMA((outs, 2, NOR)),
        ],
        compiler_params=params(20),
        cost_estimate=pl.CostEstimate(
            flops=2 * rows * GROUP_ROWS * HALF * outs, bytes_accessed=8 * MIB, transcendentals=0
        ),
        name="scores",
    )(*panels, *images)


def swap_halves(lanes, yhi):
    pieces = [
        pltpu.roll(lanes[:, k : k + 2 * ROWS], yhi * ROWS, 1)
        for k in range(0, GROUP_ROWS, 2 * ROWS)
    ]
    return jnp.concatenate(pieces, axis=1)


def norms_kernel(near_ref, near_other_ref, far_ref, far_other_ref, scores_ref, parts_ref):
    _, _, _, x, yhi = place()
    near = near_ref[...] + near_other_ref[...]
    far = far_ref[...] + far_other_ref[...]
    middle = 4 * CLS * 8
    scores = jnp.concatenate([near[:middle], far, near[middle:]], axis=0)
    scores_ref[...] = scores
    scores = scores.reshape(NZ, CLS, 8, GROUP_ROWS)
    maximum = jnp.max(jnp.max(scores, axis=0), axis=1, keepdims=True)
    totals = jnp.sum(jnp.sum(jnp.exp(scores - maximum[None]), axis=0), axis=1)
    lse = swap_halves(maximum[:, 0, :] + jnp.log(totals), yhi)
    lse = pltpu.roll(lse, x * 2 * ROWS, 1)
    parts_ref[...] = jnp.broadcast_to(lse[None], parts_ref.shape)


def norms(*scores):
    return pl.pallas_call(
        norms_kernel,
        out_shape=(
            jax.ShapeDtypeStruct((NZ * CLS * 8, GROUP_ROWS), jnp.float32),
            jax.ShapeDtypeStruct((NOR, CLS, GROUP_ROWS), jnp.float32),
        ),
        in_specs=[vmem()] * 4,
        out_specs=(vmem(), vmem()),
        compiler_params=params(24),
        name="norms",
    )(*scores)


def finish_kernel(parts_ref, scores_ref, evidence_ref, posterior_ref, mass_ref):
    z, _, _, x, yhi = place()
    parts = parts_ref[...]
    maximum = jnp.max(parts, axis=0)
    class_lse = maximum + jnp.log(jnp.sum(jnp.exp(parts - maximum[None]), axis=0))
    top = jnp.max(class_lse, axis=0, keepdims=True)
    evidence = top + jnp.log(jnp.sum(jnp.exp(class_lse - top), axis=0, keepdims=True))
    evidence_ref[...] = evidence
    posterior_ref[...] = jnp.exp(class_lse - evidence)
    here = swap_halves(pltpu.roll(evidence, ((NX - x) % NX) * 2 * ROWS, 1), yhi)
    terms = jnp.exp(scores_ref[...] - here)
    ones = jnp.ones((NDP, GROUP_ROWS), jnp.float32)
    mass = lax.dot_general(ones, terms, NT, precision=HIGH, preferred_element_type=jnp.float32)
    mass_ref[...] = pltpu.roll(mass, z * CLS * 8, 1)


def finish(parts, scores):
    return pl.pallas_call(
        finish_kernel,
        out_shape=(
            jax.ShapeDtypeStruct((1, GROUP_ROWS), jnp.float32),
            jax.ShapeDtypeStruct((CLS, GROUP_ROWS), jnp.float32),
            jax.ShapeDtypeStruct((NDP, NZ * CLS * 8), jnp.float32),
        ),
        in_specs=[vmem(), vmem()],
        out_specs=(vmem(), vmem(), vmem()),
        compiler_params=params(24),
        name="finish",
    )(parts, scores)


def together(*arrays):
    return lax.optimization_barrier(arrays)


def per_device(images, groups, panel_slots, owners, contrast, noise_weight, class_prior):
    orient = lax.axis_index("orient")
    noise = noise_weight.reshape(1, PIX)

    sent = panel(owners, class_prior, panel_slots[0], contrast, noise).reshape(NDP, 8, QUART)
    got = lax.all_to_all(sent, "dp", 0, 0)

    weighted = weigh(images, groups.reshape(ROWS, 1), contrast, noise)
    own = jnp.stack([weighted[0], other_core(weighted[1])])
    across, left, right = other_yhi(own), from_left(own), from_right(own)

    got, left, right, across = together(got, left, right, across)
    mine = pick(owners, got)
    far = [from_left(left[:1]), from_right(right[1:])]
    block = jnp.stack([mine, other_ylo(mine)]).reshape(2, CLS * 8, QUART)
    up1, down1 = from_below(block), from_above(block)
    up1, down1, across, *far = together(up1, down1, across, *far)
    far = jnp.concatenate(far, axis=0)
    left_across, right_across, far_across = from_left(across), from_right(across), other_yhi(far)
    up2, down2 = from_below(up1), from_above(down1)
    up3, down3 = from_below(up2), from_above(down2)
    up3, down3, left_across, right_across, far_across = together(
        up3, down3, left_across, right_across, far_across
    )
    last = [from_below(up3[:1]), from_above(down3[1:])]
    whole = [own, across, right, right_across, far, far_across, left, left_across]

    near = [block, down1, down2, down3, up3, up2, up1]
    (near_theirs,) = scores_of(near, whole, (1,), 7)
    near_other = other_core(near_theirs)
    (near_mine,) = scores_of(near, whole, (0,), 7)
    near_mine, *last = together(near_mine, *last)
    far_theirs, far_mine = scores_of(last, whole, (1, 0), 1)
    scores, partial = norms(near_mine, near_other, far_mine, other_core(far_theirs))
    parts = lax.all_to_all(partial, "orient", 0, 0)
    evidence, posterior, mass = finish(parts, scores)
    masses = lax.all_to_all(mass, "dp", 0, 0)
    normalise = CLS * ORI * NOR / (ROWS * NOR * NDP)
    total = jnp.sum(masses, axis=0) * normalise
    orientation_mass = total.reshape(NZ, CLS, 8).transpose(1, 0, 2).reshape(CLS, ORI)
    log_evidence = lax.dynamic_slice_in_dim(evidence[0], orient * ROWS, ROWS, 0)
    class_posterior = lax.dynamic_slice_in_dim(posterior, orient * ROWS, ROWS, 1)
    return (log_evidence, class_posterior, orientation_mass)


def solution(mesh):
    return jax.shard_map(
        per_device,
        mesh=mesh,
        in_specs=(
            P(("dp", "orient"), None),
            P(("dp", "orient")),
            P("dp", "orient", None),
            P(),
            P(),
            P(),
            P(),
        ),
        out_specs=(P(("dp", "orient")), P(None, ("dp", "orient")), P(None, "orient")),
        check_vma=False,
    )
```

```python
import functools
import jax
import jax.numpy as jnp
from jax import lax
from jax.experimental import pallas as pl
from jax.experimental.pallas import tpu as pltpu
from jax.sharding import PartitionSpec as P

NX, NZ = 4, 8
NDP, NOR = 32, 8
CLS, PIX, GRP, ORI, ROWS = 8, 4224, 64, 64, 64
FEAT = 2 * PIX
EXT = 256
COLS = FEAT + EXT
HALF = COLS // 2
QUART = COLS // 4
GROUP_ROWS = NOR * ROWS
HIGH = lax.Precision.HIGHEST
NT = (((1,), (1,)), ((), ()))
MIB = 1024 * 1024


def permute(array, move):
    pairs = []
    for dp in range(NDP):
        for orient in range(NOR):
            place = (dp // 4, (dp // 2) % 2, dp % 2, orient // 2, orient % 2)
            z, ylo, core, x, yhi = move(*place)
            target = ((z % NZ) * 4 + ylo * 2 + core) * NOR + (x % NX) * 2 + yhi
            pairs.append((dp * NOR + orient, target))
    return lax.ppermute(array, ("dp", "orient"), pairs)


def other_core(array):
    return permute(array, lambda z, ylo, core, x, yhi: (z, ylo, 1 - core, x, yhi))


def other_ylo(array):
    return permute(array, lambda z, ylo, core, x, yhi: (z, 1 - ylo, core, x, yhi))


def other_yhi(array):
    return permute(array, lambda z, ylo, core, x, yhi: (z, ylo, core, x, 1 - yhi))


def from_below(array):
    return permute(array, lambda z, ylo, core, x, yhi: (z + 1, ylo, core, x, yhi))


def from_above(array):
    return permute(array, lambda z, ylo, core, x, yhi: (z - 1, ylo, core, x, yhi))


def from_left(array):
    return permute(array, lambda z, ylo, core, x, yhi: (z, ylo, core, x + 1, yhi))


def from_right(array):
    return permute(array, lambda z, ylo, core, x, yhi: (z, ylo, core, x - 1, yhi))


def vmem():
    return pl.BlockSpec(memory_space=pltpu.VMEM)


def anywhere():
    return pl.BlockSpec(memory_space=pl.ANY)


def smem():
    return pl.BlockSpec(memory_space=pltpu.SMEM)


def params(mib, **more):
    return pltpu.CompilerParams(vmem_limit_bytes=mib * MIB, **more)


def place():
    dp, orient = lax.axis_index("dp"), lax.axis_index("orient")
    return dp // 4, (dp // 2) % 2, dp % 2, orient // 2, orient % 2


def weigh_kernel(images_ref, groups_ref, contrast_ref, noise_ref, out_ref):
    _, ylo, core, _, _ = place()
    hot = (
        groups_ref[...] == lax.broadcasted_iota(jnp.int32, (ROWS, GRP), 1)
    ).astype(jnp.float32)
    rows = jnp.dot(hot, contrast_ref[...], precision=HIGH, preferred_element_type=jnp.float32)
    factor = rows * noise_ref[...]
    real = (images_ref[:, :PIX].astype(jnp.float32) * factor).astype(jnp.bfloat16)
    imag = (images_ref[:, PIX:].astype(jnp.float32) * factor).astype(jnp.bfloat16)
    ext = jnp.concatenate([hot, hot, hot, jnp.zeros_like(hot)], axis=1).astype(jnp.bfloat16)
    out_ref[core, ylo] = real[:, :QUART]
    out_ref[core, 1 - ylo] = jnp.concatenate([real[:, QUART:], imag[:, : HALF - PIX]], axis=1)
    out_ref[1 - core, ylo] = imag[:, HALF - PIX : 3 * QUART - PIX]
    out_ref[1 - core, 1 - ylo] = jnp.concatenate([imag[:, 3 * QUART - PIX :], ext], axis=1)


def weigh(images, groups, contrast, noise):
    return pl.pallas_call(
        weigh_kernel,
        out_shape=jax.ShapeDtypeStruct((2, 2, ROWS, QUART), jnp.bfloat16),
        in_specs=[vmem(), vmem(), vmem(), vmem()],
        out_specs=vmem(),
        compiler_params=params(24),
        name="weigh",
    )(images, groups, contrast, noise)


def panel_kernel(
    owners_hbm, priors_hbm, slot_hbm, contrast_hbm, noise_hbm, out_ref,
    owners_ref, priors_ref, slot_ref, contrast_ref, noise_ref, sems,
):
    pairs = [
        (slot_hbm.at[0], slot_ref),
        (contrast_hbm, contrast_ref),
        (noise_hbm, noise_ref),
        (owners_hbm, owners_ref),
        (priors_hbm, priors_ref),
    ]
    copies = [pltpu.make_async_copy(a, b, sems.at[k]) for k, (a, b) in enumerate(pairs)]
    for copy in copies:
        copy.start()

    def chunks(ylo, ext):
        for z in range(NZ):
            rows = slice(8 * z, 8 * z + 8)
            parts = []
            for core in range(2):
                start = core * HALF + ylo * QUART
                stop = min(start + QUART, FEAT)
                part = slot_ref[:, start:stop].astype(jnp.float32)[rows]
                if stop < start + QUART:
                    part = jnp.concatenate([part, ext[rows]], axis=1)
                parts.append(part)
            at = (z * 4 + ylo * 2) * 8
            out_ref[at : at + 16, :] = jnp.concatenate(parts, axis=0).astype(jnp.bfloat16)

    copies[0].wait()
    chunks(0, None)
    for copy in copies[1:]:
        copy.wait()
    dp = lax.axis_index("dp")
    prior = jnp.float32(0)
    for k in range(CLS):
        prior += jnp.where(owners_ref[k] == dp, priors_ref[k], jnp.float32(0))
    contrast = contrast_ref[...]
    power = contrast * contrast * noise_ref[...].reshape(1, PIX)
    real = slot_ref[:, :PIX].astype(jnp.float32)
    imag = slot_ref[:, PIX:].astype(jnp.float32)
    table = lax.dot_general(
        real * real + imag * imag, power, NT, precision=HIGH, preferred_element_type=jnp.float32
    )
    table = -0.5 * table + prior
    first = table.astype(jnp.bfloat16).astype(jnp.float32)
    rest = table - first
    second = rest.astype(jnp.bfloat16).astype(jnp.float32)
    third = rest - second
    chunks(1, jnp.concatenate([first, second, third, jnp.zeros_like(first)], axis=1))


def panel(owners, priors, slots, contrast, noise):
    return pl.pallas_call(
        panel_kernel,
        out_shape=jax.ShapeDtypeStruct((NDP * 8, QUART), jnp.bfloat16),
        in_specs=[anywhere()] * 5,
        out_specs=vmem(),
        scratch_shapes=[
            pltpu.SMEM((CLS,), jnp.int32),
            pltpu.SMEM((CLS,), jnp.float32),
            pltpu.VMEM((ROWS, FEAT), jnp.bfloat16),
            pltpu.VMEM((GRP, PIX), jnp.float32),
            pltpu.VMEM((PIX,), jnp.float32),
            pltpu.SemaphoreType.DMA((5,)),
        ],
        compiler_params=params(60),
        name="panel",
    )(owners, priors, slots, contrast, noise)


def pick_kernel(owners_ref, got_ref, out_ref, sems):
    copies = [
        pltpu.make_async_copy(got_ref.at[owners_ref[k]], out_ref.at[k], sems.at[k])
        for k in range(CLS)
    ]
    for copy in copies:
        copy.start()
    for copy in copies:
        copy.wait()


def pick(owners, got):
    return pl.pallas_call(
        pick_kernel,
        out_shape=jax.ShapeDtypeStruct((CLS, 8, QUART), jnp.bfloat16),
        in_specs=[smem(), anywhere()],
        out_specs=vmem(),
        scratch_shapes=[pltpu.SemaphoreType.DMA((CLS,))],
        compiler_params=params(16),
        name="pick",
    )(owners, got)


def scores_kernel(owners, plan, *refs):
    n_panels = sum(count for _, count, _ in plan)
    panels, images, outs = refs[:n_panels], refs[n_panels : n_panels + NOR], refs[n_panels + NOR :]
    at = 0
    for chain, count, first in plan:
        panel = jnp.concatenate([ref[...] for ref in panels[at : at + count]], axis=0)
        for owner, out in zip(owners, outs):
            image = jnp.concatenate([ref[owner, chain] for ref in images], axis=0)
            part = lax.dot_general(panel, image, NT, preferred_element_type=jnp.float32)
            if at == 0:
                out[...] = part
            else:
                out[first : first + panel.shape[0]] += part
        at += count


def scores_of(panels, images, owners, plan):
    rows = plan[0][1] * CLS * 8
    outs = len(owners)
    return pl.pallas_call(
        functools.partial(scores_kernel, owners, plan),
        out_shape=[jax.ShapeDtypeStruct((rows, GROUP_ROWS), jnp.float32)] * outs,
        in_specs=[vmem()] * (len(panels) + NOR),
        out_specs=[vmem()] * outs,
        compiler_params=params(16),
        cost_estimate=pl.CostEstimate(
            flops=2 * len(panels) * CLS * 8 * GROUP_ROWS * QUART * outs,
            bytes_accessed=8 * MIB,
            transcendentals=0,
        ),
        name="scores",
    )(*panels, *images)


def swap_halves(lanes, yhi):
    pieces = [
        pltpu.roll(lanes[:, k : k + 2 * ROWS], yhi * ROWS, 1)
        for k in range(0, GROUP_ROWS, 2 * ROWS)
    ]
    return jnp.concatenate(pieces, axis=1)


def norms_kernel(near_ref, near_other_ref, far_ref, far_other_ref, scores_ref, parts_ref):
    _, _, _, x, yhi = place()
    near = near_ref[...] + near_other_ref[...]
    far = far_ref[...] + far_other_ref[...]
    step = CLS * 8
    full, part = 5 * step, 7 * step
    third = near[full : full + step] + far[:step]
    fifth = near[full + step : part] + far[step : 2 * step]
    scores = jnp.concatenate(
        [near[: 3 * step], third, far[2 * step :], fifth, near[3 * step : full]], axis=0
    )
    scores_ref[...] = scores
    scores = scores.reshape(NZ, CLS, 8, GROUP_ROWS)
    maximum = jnp.max(jnp.max(scores, axis=0), axis=1, keepdims=True)
    totals = jnp.sum(jnp.sum(jnp.exp(scores - maximum[None]), axis=0), axis=1)
    lse = swap_halves(maximum[:, 0, :] + jnp.log(totals), yhi)
    lse = pltpu.roll(lse, x * 2 * ROWS, 1)
    parts_ref[...] = jnp.broadcast_to(lse[None], parts_ref.shape)


def norms(*scores):
    return pl.pallas_call(
        norms_kernel,
        out_shape=(
            jax.ShapeDtypeStruct((NZ * CLS * 8, GROUP_ROWS), jnp.float32),
            jax.ShapeDtypeStruct((NOR, CLS, GROUP_ROWS), jnp.float32),
        ),
        in_specs=[vmem()] * 4,
        out_specs=(vmem(), vmem()),
        compiler_params=params(24),
        name="norms",
    )(*scores)


def finish_kernel(parts_ref, scores_ref, evidence_ref, posterior_ref, mass_ref):
    z, _, _, x, yhi = place()
    parts = parts_ref[...]
    maximum = jnp.max(parts, axis=0)
    class_lse = maximum + jnp.log(jnp.sum(jnp.exp(parts - maximum[None]), axis=0))
    top = jnp.max(class_lse, axis=0, keepdims=True)
    evidence = top + jnp.log(jnp.sum(jnp.exp(class_lse - top), axis=0, keepdims=True))
    evidence_ref[...] = evidence
    posterior_ref[...] = jnp.exp(class_lse - evidence)
    here = swap_halves(pltpu.roll(evidence, ((NX - x) % NX) * 2 * ROWS, 1), yhi)
    terms = jnp.exp(scores_ref[...] - here)
    ones = jnp.ones((NDP, GROUP_ROWS), jnp.float32)
    mass = lax.dot_general(ones, terms, NT, precision=HIGH, preferred_element_type=jnp.float32)
    mass_ref[...] = pltpu.roll(mass, z * CLS * 8, 1).reshape(mass_ref.shape)


def finish(parts, scores):
    return pl.pallas_call(
        finish_kernel,
        out_shape=(
            jax.ShapeDtypeStruct((1, GROUP_ROWS), jnp.float32),
            jax.ShapeDtypeStruct((CLS, GROUP_ROWS), jnp.float32),
            jax.ShapeDtypeStruct((NDP, 1, NZ * CLS * 8), jnp.float32),
        ),
        in_specs=[vmem(), vmem()],
        out_specs=(vmem(), vmem(), vmem()),
        compiler_params=params(24),
        name="finish",
    )(parts, scores)


def together(*arrays):
    return lax.optimization_barrier(arrays)


def per_device(images, groups, panel_slots, owners, contrast, noise_weight, class_prior):
    orient = lax.axis_index("orient")
    noise = noise_weight.reshape(1, PIX)

    sent = panel(owners, class_prior, panel_slots, contrast, noise_weight).reshape(NDP, 8, QUART)
    got = lax.all_to_all(sent, "dp", 0, 0)

    weighted = weigh(images, groups.reshape(ROWS, 1), contrast, noise)
    own = jnp.stack([weighted[0], other_core(weighted[1])])
    left, right, across = from_left(own), from_right(own), other_yhi(own)

    got, left, right = together(got, left, right)
    far = [from_left(left[:1]), from_right(right[1:])]
    mine0 = pick(owners, got).reshape(CLS * 8, QUART)
    mine1, mine7 = from_above(mine0), from_below(mine0)
    theirs0 = other_ylo(mine0)

    mine1, mine7, theirs0, across, *far = together(mine1, mine7, theirs0, across, *far)
    pair1 = from_above(jnp.stack([mine1, theirs0]))
    pair7 = from_below(jnp.stack([mine7, theirs0]))
    far = jnp.concatenate(far, axis=0)
    left_across, right_across, far_across = from_left(across), from_right(across), other_yhi(far)
    mine2, theirs1 = pair1
    mine6, theirs7 = pair7
    pair2, pair6 = from_above(pair1), from_below(pair7)

    pair2, pair6, left_across, right_across, far_across = together(
        pair2, pair6, left_across, right_across, far_across
    )
    mine3, theirs2 = pair2
    mine5, theirs6 = pair6
    half = CLS * 4
    next3 = from_above(jnp.concatenate([mine3[half:], theirs2], axis=0))
    next5 = from_below(jnp.concatenate([mine5[:half], theirs6], axis=0))
    whole = [own, across, right, right_across, far, far_across, left, left_across]
    near = [mine0, mine1, mine2, mine6, mine7, mine3, mine5]
    near += [theirs0, theirs1, theirs2, theirs6, theirs7]
    near_plan = ((0, 7, 0), (1, 5, 0))
    (near_theirs,) = scores_of(near, whole, (1,), near_plan)
    near_other = other_core(near_theirs)
    (near_mine,) = scores_of(near, whole, (0,), near_plan)
    theirs3, theirs5 = next3[half:], next5[half:]
    last = [from_below(theirs5[:half]), from_above(theirs3[half:])]
    near_mine, *last = together(near_mine, *last)
    mine4 = jnp.concatenate([next5[:half], next3[:half]], axis=0)
    theirs4 = jnp.concatenate(last, axis=0)
    far_theirs, far_mine = scores_of(
        [theirs3, theirs5, theirs4, mine4], whole, (1, 0), ((1, 3, 0), (0, 1, 2 * CLS * 8))
    )
    scores, partial = norms(near_mine, near_other, far_mine, other_core(far_theirs))
    parts = lax.all_to_all(partial, "orient", 0, 0)
    evidence, posterior, mass = finish(parts, scores)
    masses = lax.all_to_all(mass, "dp", 0, 0)
    normalise = CLS * ORI * NOR / (ROWS * NOR * NDP)
    total = jnp.sum(masses, axis=(0, 1)) * normalise
    orientation_mass = total.reshape(NZ, CLS, 8).transpose(1, 0, 2).reshape(CLS, ORI)
    log_evidence = lax.dynamic_slice_in_dim(evidence[0], orient * ROWS, ROWS, 0)
    class_posterior = lax.dynamic_slice_in_dim(posterior, orient * ROWS, ROWS, 1)
    return (log_evidence, class_posterior, orientation_mass)


def solution(mesh):
    return jax.shard_map(
        per_device,
        mesh=mesh,
        in_specs=(
            P(("dp", "orient"), None),
            P(("dp", "orient")),
            P("dp", "orient", None),
            P(),
            P(),
            P(),
            P(),
        ),
        out_specs=(P(("dp", "orient")), P(None, ("dp", "orient")), P(None, "orient")),
        check_vma=False,
    )
```

```python
import functools
import jax
import jax.numpy as jnp
from jax import lax
from jax.experimental import pallas as pl
from jax.experimental.pallas import tpu as pltpu
from jax.sharding import PartitionSpec as P

NX, NZ = 4, 8
NDP, NOR = 32, 8
CLS, PIX, GRP, ORI, ROWS = 8, 4224, 64, 64, 64
FEAT = 2 * PIX
EXT = 256
COLS = FEAT + EXT
HALF = COLS // 2
QUART = COLS // 4
GROUP_ROWS = NOR * ROWS
HIGH = lax.Precision.HIGHEST
NT = (((1,), (1,)), ((), ()))
MIB = 1024 * 1024


def permute(array, move):
    pairs = []
    for dp in range(NDP):
        for orient in range(NOR):
            place = (dp // 4, (dp // 2) % 2, dp % 2, orient // 2, orient % 2)
            z, ylo, core, x, yhi = move(*place)
            target = ((z % NZ) * 4 + ylo * 2 + core) * NOR + (x % NX) * 2 + yhi
            pairs.append((dp * NOR + orient, target))
    return lax.ppermute(array, ("dp", "orient"), pairs)


def other_core(array):
    return permute(array, lambda z, ylo, core, x, yhi: (z, ylo, 1 - core, x, yhi))


def other_ylo(array):
    return permute(array, lambda z, ylo, core, x, yhi: (z, 1 - ylo, core, x, yhi))


def other_yhi(array):
    return permute(array, lambda z, ylo, core, x, yhi: (z, ylo, core, x, 1 - yhi))


def from_below(array):
    return permute(array, lambda z, ylo, core, x, yhi: (z + 1, ylo, core, x, yhi))


def from_above(array):
    return permute(array, lambda z, ylo, core, x, yhi: (z - 1, ylo, core, x, yhi))


def from_left(array):
    return permute(array, lambda z, ylo, core, x, yhi: (z, ylo, core, x + 1, yhi))


def from_right(array):
    return permute(array, lambda z, ylo, core, x, yhi: (z, ylo, core, x - 1, yhi))


def vmem():
    return pl.BlockSpec(memory_space=pltpu.VMEM)


def anywhere():
    return pl.BlockSpec(memory_space=pl.ANY)


def smem():
    return pl.BlockSpec(memory_space=pltpu.SMEM)


def params(mib, **more):
    return pltpu.CompilerParams(vmem_limit_bytes=mib * MIB, **more)


def place():
    dp, orient = lax.axis_index("dp"), lax.axis_index("orient")
    return dp // 4, (dp // 2) % 2, dp % 2, orient // 2, orient % 2


def weigh_kernel(images_ref, groups_ref, contrast_ref, noise_ref, out_ref):
    _, ylo, core, _, _ = place()
    hot = (
        groups_ref[...] == lax.broadcasted_iota(jnp.int32, (ROWS, GRP), 1)
    ).astype(jnp.float32)
    rows = jnp.dot(hot, contrast_ref[...], precision=HIGH, preferred_element_type=jnp.float32)
    factor = rows * noise_ref[...]
    real = (images_ref[:, :PIX].astype(jnp.float32) * factor).astype(jnp.bfloat16)
    imag = (images_ref[:, PIX:].astype(jnp.float32) * factor).astype(jnp.bfloat16)
    ext = jnp.concatenate([hot, hot, hot, jnp.zeros_like(hot)], axis=1).astype(jnp.bfloat16)
    out_ref[core, ylo] = real[:, :QUART]
    out_ref[core, 1 - ylo] = jnp.concatenate([real[:, QUART:], imag[:, : HALF - PIX]], axis=1)
    out_ref[1 - core, ylo] = imag[:, HALF - PIX : 3 * QUART - PIX]
    out_ref[1 - core, 1 - ylo] = jnp.concatenate([imag[:, 3 * QUART - PIX :], ext], axis=1)


def weigh(images, groups, contrast, noise):
    return pl.pallas_call(
        weigh_kernel,
        out_shape=jax.ShapeDtypeStruct((2, 2, ROWS, QUART), jnp.bfloat16),
        in_specs=[vmem(), vmem(), vmem(), vmem()],
        out_specs=vmem(),
        compiler_params=params(24),
        name="weigh",
    )(images, groups, contrast, noise)


def panel_kernel(
    owners_hbm, priors_hbm, slot_hbm, contrast_hbm, noise_hbm, out_ref,
    owners_ref, priors_ref, slot_ref, contrast_ref, noise_ref, sems,
):
    pairs = [
        (slot_hbm.at[0], slot_ref),
        (contrast_hbm, contrast_ref),
        (noise_hbm, noise_ref),
        (owners_hbm, owners_ref),
        (priors_hbm, priors_ref),
    ]
    copies = [pltpu.make_async_copy(a, b, sems.at[k]) for k, (a, b) in enumerate(pairs)]
    for copy in copies:
        copy.start()

    def chunks(ylo, ext):
        for z in range(NZ):
            rows = slice(8 * z, 8 * z + 8)
            parts = []
            for core in range(2):
                start = core * HALF + ylo * QUART
                stop = min(start + QUART, FEAT)
                part = slot_ref[:, start:stop].astype(jnp.float32)[rows]
                if stop < start + QUART:
                    part = jnp.concatenate([part, ext[rows]], axis=1)
                parts.append(part)
            at = (z * 4 + ylo * 2) * 8
            out_ref[at : at + 16, :] = jnp.concatenate(parts, axis=0).astype(jnp.bfloat16)

    copies[0].wait()
    chunks(0, None)
    for copy in copies[1:]:
        copy.wait()
    dp = lax.axis_index("dp")
    prior = jnp.float32(0)
    for k in range(CLS):
        prior += jnp.where(owners_ref[k] == dp, priors_ref[k], jnp.float32(0))
    contrast = contrast_ref[...]
    power = contrast * contrast * noise_ref[...].reshape(1, PIX)
    real = slot_ref[:, :PIX].astype(jnp.float32)
    imag = slot_ref[:, PIX:].astype(jnp.float32)
    table = lax.dot_general(
        real * real + imag * imag, power, NT, precision=HIGH, preferred_element_type=jnp.float32
    )
    table = -0.5 * table + prior
    first = table.astype(jnp.bfloat16).astype(jnp.float32)
    rest = table - first
    second = rest.astype(jnp.bfloat16).astype(jnp.float32)
    third = rest - second
    chunks(1, jnp.concatenate([first, second, third, jnp.zeros_like(first)], axis=1))


def panel(owners, priors, slots, contrast, noise):
    return pl.pallas_call(
        panel_kernel,
        out_shape=jax.ShapeDtypeStruct((NDP * 8, QUART), jnp.bfloat16),
        in_specs=[anywhere()] * 5,
        out_specs=vmem(),
        scratch_shapes=[
            pltpu.SMEM((CLS,), jnp.int32),
            pltpu.SMEM((CLS,), jnp.float32),
            pltpu.VMEM((ROWS, FEAT), jnp.bfloat16),
            pltpu.VMEM((GRP, PIX), jnp.float32),
            pltpu.VMEM((PIX,), jnp.float32),
            pltpu.SemaphoreType.DMA((5,)),
        ],
        compiler_params=params(60),
        name="panel",
    )(owners, priors, slots, contrast, noise)


def pick_kernel(owners_ref, got_ref, out_ref, sems):
    copies = [
        pltpu.make_async_copy(got_ref.at[owners_ref[k]], out_ref.at[k], sems.at[k])
        for k in range(CLS)
    ]
    for copy in copies:
        copy.start()
    for copy in copies:
        copy.wait()


def pick(owners, got):
    return pl.pallas_call(
        pick_kernel,
        out_shape=jax.ShapeDtypeStruct((CLS, 8, QUART), jnp.bfloat16),
        in_specs=[smem(), anywhere()],
        out_specs=vmem(),
        scratch_shapes=[pltpu.SemaphoreType.DMA((CLS,))],
        compiler_params=params(16),
        name="pick",
    )(owners, got)


def settle_kernel(in_ref, out_ref, sem):
    copy = pltpu.make_async_copy(in_ref, out_ref, sem)
    copy.start()
    copy.wait()


def settle(array):
    return pl.pallas_call(
        settle_kernel,
        out_shape=jax.ShapeDtypeStruct(array.shape, array.dtype),
        in_specs=[anywhere()],
        out_specs=vmem(),
        scratch_shapes=[pltpu.SemaphoreType.DMA],
        compiler_params=params(16),
        name="settle",
    )(array)


def scores_kernel(owners, plan, *refs):
    n_panels = sum(count for _, count, _ in plan)
    panels, images, outs = refs[:n_panels], refs[n_panels : n_panels + NOR], refs[n_panels + NOR :]
    at = 0
    for chain, count, first in plan:
        panel = jnp.concatenate([ref[...] for ref in panels[at : at + count]], axis=0)
        for owner, out in zip(owners, outs):
            image = jnp.concatenate([ref[owner, chain] for ref in images], axis=0)
            part = lax.dot_general(panel, image, NT, preferred_element_type=jnp.float32)
            if at == 0:
                out[...] = part
            else:
                out[first : first + panel.shape[0]] += part
        at += count


def scores_of(panels, images, owners, plan):
    rows = plan[0][1] * CLS * 8
    outs = len(owners)
    return pl.pallas_call(
        functools.partial(scores_kernel, owners, plan),
        out_shape=[jax.ShapeDtypeStruct((rows, GROUP_ROWS), jnp.float32)] * outs,
        in_specs=[vmem()] * (len(panels) + NOR),
        out_specs=[vmem()] * outs,
        compiler_params=params(16),
        cost_estimate=pl.CostEstimate(
            flops=2 * len(panels) * CLS * 8 * GROUP_ROWS * QUART * outs,
            bytes_accessed=8 * MIB,
            transcendentals=0,
        ),
        name="scores",
    )(*panels, *images)


def swap_halves(lanes, yhi):
    pieces = [
        pltpu.roll(lanes[:, k : k + 2 * ROWS], yhi * ROWS, 1)
        for k in range(0, GROUP_ROWS, 2 * ROWS)
    ]
    return jnp.concatenate(pieces, axis=1)


def norms_kernel(near_ref, near_other_ref, far_ref, far_other_ref, scores_ref, parts_ref):
    _, _, _, x, yhi = place()
    near = near_ref[...] + near_other_ref[...]
    far = far_ref[...] + far_other_ref[...]
    step = CLS * 8
    rows = [near[k : k + step] for k in range(0, NZ * step, step)]
    for k in range(3):
        rows[5 + k] += far[k * step : (k + 1) * step]
    scores = jnp.concatenate([rows[k] for k in (0, 1, 2, 5, 7, 6, 3, 4)], axis=0)
    scores_ref[...] = scores
    scores = scores.reshape(NZ, CLS, 8, GROUP_ROWS)
    maximum = jnp.max(jnp.max(scores, axis=0), axis=1, keepdims=True)
    totals = jnp.sum(jnp.sum(jnp.exp(scores - maximum[None]), axis=0), axis=1)
    lse = swap_halves(maximum[:, 0, :] + jnp.log(totals), yhi)
    lse = pltpu.roll(lse, x * 2 * ROWS, 1)
    parts_ref[...] = jnp.broadcast_to(lse[None], parts_ref.shape)


def norms(*scores):
    return pl.pallas_call(
        norms_kernel,
        out_shape=(
            jax.ShapeDtypeStruct((NZ * CLS * 8, GROUP_ROWS), jnp.float32),
            jax.ShapeDtypeStruct((NOR, CLS, GROUP_ROWS), jnp.float32),
        ),
        in_specs=[vmem()] * 4,
        out_specs=(vmem(), vmem()),
        compiler_params=params(24),
        name="norms",
    )(*scores)


def finish_kernel(parts_ref, scores_ref, evidence_ref, posterior_ref, mass_ref):
    z, _, _, x, yhi = place()
    parts = parts_ref[...]
    maximum = jnp.max(parts, axis=0)
    class_lse = maximum + jnp.log(jnp.sum(jnp.exp(parts - maximum[None]), axis=0))
    top = jnp.max(class_lse, axis=0, keepdims=True)
    evidence = top + jnp.log(jnp.sum(jnp.exp(class_lse - top), axis=0, keepdims=True))
    evidence_ref[...] = evidence
    posterior_ref[...] = jnp.exp(class_lse - evidence)
    here = swap_halves(pltpu.roll(evidence, ((NX - x) % NX) * 2 * ROWS, 1), yhi)
    terms = jnp.exp(scores_ref[...] - here)
    ones = jnp.ones((8, GROUP_ROWS), jnp.float32)
    mass = lax.dot_general(ones, terms, NT, precision=HIGH, preferred_element_type=jnp.float32)
    mass = pltpu.roll(mass, z * CLS * 8, 1)[:1]
    for k in range(NDP):
        mass_ref[k] = mass


def finish(parts, scores):
    return pl.pallas_call(
        finish_kernel,
        out_shape=(
            jax.ShapeDtypeStruct((1, GROUP_ROWS), jnp.float32),
            jax.ShapeDtypeStruct((CLS, GROUP_ROWS), jnp.float32),
            jax.ShapeDtypeStruct((NDP, 1, NZ * CLS * 8), jnp.float32),
        ),
        in_specs=[vmem(), vmem()],
        out_specs=(vmem(), vmem(), vmem()),
        compiler_params=params(24),
        name="finish",
    )(parts, scores)


def together(*arrays):
    return lax.optimization_barrier(arrays)


def per_device(images, groups, panel_slots, owners, contrast, noise_weight, class_prior):
    orient = lax.axis_index("orient")
    noise = noise_weight.reshape(1, PIX)

    sent = panel(owners, class_prior, panel_slots, contrast, noise_weight).reshape(NDP, 8, QUART)
    sent, images = together(sent, images)
    got = lax.all_to_all(sent, "dp", 0, 0)

    weighted = weigh(images, groups.reshape(ROWS, 1), contrast, noise)
    own = jnp.stack([weighted[0], other_core(weighted[1])])
    across, left, right = other_yhi(own), from_left(own), from_right(own)

    got, left, right = together(got, left, right)
    half = CLS * 4
    mine0 = pick(owners, got).reshape(CLS * 8, QUART)
    mine1, mine7 = from_above(mine0), from_below(mine0)
    theirs0 = other_ylo(mine0)
    left, _ = together(left, mine0)
    far0 = from_left(left[:1])
    mine1, mine7, across, right = together(mine1, mine7, across, right)
    far1 = from_right(right[1:])
    mine2, mine6 = from_above(mine1), from_below(mine7)
    mine2, mine6, theirs0 = together(mine2, mine6, theirs0)
    pair3 = from_above(jnp.stack([mine2, theirs0]))
    pair5 = from_below(jnp.stack([mine6, theirs0]))
    far0, far1, across = together(far0, far1, across)
    far = jnp.concatenate([far0, far1], axis=0)
    left_across, right_across, far_across = from_left(across), from_right(across), other_yhi(far)
    pair3, pair5 = together(pair3, pair5)
    mine3, theirs1 = pair3
    mine5, theirs7 = pair5
    next4 = from_above(jnp.concatenate([mine3[half:], theirs1], axis=0))
    next6 = from_below(jnp.concatenate([mine5[:half], theirs7], axis=0))
    next4, next6 = together(next4, next6)
    theirs2, theirs6 = next4[half:], next6[half:]
    mine4 = jnp.concatenate([next6[:half], next4[:half]], axis=0)
    theirs3, theirs5 = from_above(theirs2), from_below(theirs6)
    across = settle(across)
    whole = [own, across, right, right_across, far, far_across, left, left_across]
    near = [mine0, mine1, mine2, mine6, mine7, mine3, mine5, mine4]
    near += [theirs0, theirs1, theirs2, theirs6, theirs7]
    near_plan = ((0, 8, 0), (1, 5, 0))
    (near_theirs,) = scores_of(near, whole, (1,), near_plan)
    near_other = other_core(near_theirs)
    (near_mine,) = scores_of(near, whole, (0,), near_plan)
    last = [from_below(theirs5[:half]), from_above(theirs3[half:])]
    near_mine, *last = together(near_mine, *last)
    far_panels, far_plan = [theirs3, theirs5, jnp.concatenate(last, axis=0)], ((1, 3, 0),)
    (far_theirs,) = scores_of(far_panels, whole, (1,), far_plan)
    far_other = other_core(far_theirs)
    (far_mine,) = scores_of(far_panels, whole, (0,), far_plan)
    scores, partial = norms(near_mine, near_other, far_mine, far_other)
    parts = lax.all_to_all(partial, "orient", 0, 0)
    evidence, posterior, mass = finish(parts, scores)
    masses = lax.all_to_all(mass, "dp", 0, 0)
    normalise = CLS * ORI * NOR / (ROWS * NOR * NDP)
    total = jnp.sum(masses, axis=(0, 1)) * normalise
    orientation_mass = total.reshape(NZ, CLS, 8).transpose(1, 0, 2).reshape(CLS, ORI)
    log_evidence = lax.dynamic_slice_in_dim(evidence[0], orient * ROWS, ROWS, 0)
    class_posterior = lax.dynamic_slice_in_dim(posterior, orient * ROWS, ROWS, 1)
    return (log_evidence, class_posterior, orientation_mass)


def solution(mesh):
    return jax.shard_map(
        per_device,
        mesh=mesh,
        in_specs=(
            P(("dp", "orient"), None),
            P(("dp", "orient")),
            P("dp", "orient", None),
            P(),
            P(),
            P(),
            P(),
        ),
        out_specs=(P(("dp", "orient")), P(None, ("dp", "orient")), P(None, "orient")),
        check_vma=False,
    )
```

```python
import functools
import jax
import jax.numpy as jnp
from jax import lax
from jax.experimental import pallas as pl
from jax.experimental.pallas import tpu as pltpu
from jax.sharding import PartitionSpec as P

NX, NZ = 4, 8
NDP, NOR = 32, 8
CLS, PIX, GRP, ORI, ROWS = 8, 4224, 64, 64, 64
FEAT = 2 * PIX
EXT = 256
COLS = FEAT + EXT
HALF = COLS // 2
QUART = COLS // 4
GROUP_ROWS = NOR * ROWS
HIGH = lax.Precision.HIGHEST
NT = (((1,), (1,)), ((), ()))
MIB = 1024 * 1024


def permute(array, move):
    pairs = []
    for dp in range(NDP):
        for orient in range(NOR):
            place = (dp // 4, (dp // 2) % 2, dp % 2, orient // 2, orient % 2)
            z, ylo, core, x, yhi = move(*place)
            target = ((z % NZ) * 4 + ylo * 2 + core) * NOR + (x % NX) * 2 + yhi
            pairs.append((dp * NOR + orient, target))
    return lax.ppermute(array, ("dp", "orient"), pairs)


def other_core(array):
    return permute(array, lambda z, ylo, core, x, yhi: (z, ylo, 1 - core, x, yhi))


def other_ylo(array):
    return permute(array, lambda z, ylo, core, x, yhi: (z, 1 - ylo, core, x, yhi))


def other_yhi(array):
    return permute(array, lambda z, ylo, core, x, yhi: (z, ylo, core, x, 1 - yhi))


def from_below(array):
    return permute(array, lambda z, ylo, core, x, yhi: (z + 1, ylo, core, x, yhi))


def from_above(array):
    return permute(array, lambda z, ylo, core, x, yhi: (z - 1, ylo, core, x, yhi))


def both_ways_along_x(array):
    return permute(
        array, lambda z, ylo, core, x, yhi: (z, ylo, core, x + 1 - 2 * core, yhi)
    )


def from_left(array):
    return permute(array, lambda z, ylo, core, x, yhi: (z, ylo, core, x + 1, yhi))


def from_right(array):
    return permute(array, lambda z, ylo, core, x, yhi: (z, ylo, core, x - 1, yhi))


def vmem():
    return pl.BlockSpec(memory_space=pltpu.VMEM)


def anywhere():
    return pl.BlockSpec(memory_space=pl.ANY)


def smem():
    return pl.BlockSpec(memory_space=pltpu.SMEM)


def params(mib, **more):
    return pltpu.CompilerParams(vmem_limit_bytes=mib * MIB, **more)


def place():
    dp, orient = lax.axis_index("dp"), lax.axis_index("orient")
    return dp // 4, (dp // 2) % 2, dp % 2, orient // 2, orient % 2


def weigh_kernel(images_ref, groups_ref, contrast_ref, noise_ref, out_ref):
    _, ylo, core, _, _ = place()
    hot = (
        groups_ref[...] == lax.broadcasted_iota(jnp.int32, (ROWS, GRP), 1)
    ).astype(jnp.float32)
    rows = jnp.dot(hot, contrast_ref[...], precision=HIGH, preferred_element_type=jnp.float32)
    factor = rows * noise_ref[...]
    real = (images_ref[:, :PIX].astype(jnp.float32) * factor).astype(jnp.bfloat16)
    imag = (images_ref[:, PIX:].astype(jnp.float32) * factor).astype(jnp.bfloat16)
    ext = jnp.concatenate([hot, hot, hot, jnp.zeros_like(hot)], axis=1).astype(jnp.bfloat16)
    out_ref[core, ylo] = real[:, :QUART]
    out_ref[core, 1 - ylo] = jnp.concatenate([real[:, QUART:], imag[:, : HALF - PIX]], axis=1)
    out_ref[1 - core, ylo] = imag[:, HALF - PIX : 3 * QUART - PIX]
    out_ref[1 - core, 1 - ylo] = jnp.concatenate([imag[:, 3 * QUART - PIX :], ext], axis=1)


def weigh(images, groups, contrast, noise):
    return pl.pallas_call(
        weigh_kernel,
        out_shape=jax.ShapeDtypeStruct((2, 2, ROWS, QUART), jnp.bfloat16),
        in_specs=[vmem(), vmem(), vmem(), vmem()],
        out_specs=vmem(),
        compiler_params=params(24),
        name="weigh",
    )(images, groups, contrast, noise)


def panel_kernel(
    owners_hbm, priors_hbm, slot_hbm, contrast_hbm, noise_hbm, out_ref,
    owners_ref, priors_ref, slot_ref, contrast_ref, noise_ref, sems,
):
    pairs = [
        (slot_hbm.at[0], slot_ref),
        (contrast_hbm, contrast_ref),
        (noise_hbm, noise_ref),
        (owners_hbm, owners_ref),
        (priors_hbm, priors_ref),
    ]
    copies = [pltpu.make_async_copy(a, b, sems.at[k]) for k, (a, b) in enumerate(pairs)]
    for copy in copies:
        copy.start()

    def chunks(ylo, ext):
        for z in range(NZ):
            rows = slice(8 * z, 8 * z + 8)
            parts = []
            for core in range(2):
                start = core * HALF + ylo * QUART
                stop = min(start + QUART, FEAT)
                part = slot_ref[:, start:stop].astype(jnp.float32)[rows]
                if stop < start + QUART:
                    part = jnp.concatenate([part, ext[rows]], axis=1)
                parts.append(part)
            at = (z * 4 + ylo * 2) * 8
            out_ref[at : at + 16, :] = jnp.concatenate(parts, axis=0).astype(jnp.bfloat16)

    copies[0].wait()
    chunks(0, None)
    for copy in copies[1:]:
        copy.wait()
    dp = lax.axis_index("dp")
    prior = jnp.float32(0)
    for k in range(CLS):
        prior += jnp.where(owners_ref[k] == dp, priors_ref[k], jnp.float32(0))
    contrast = contrast_ref[...]
    power = contrast * contrast * noise_ref[...].reshape(1, PIX)
    real = slot_ref[:, :PIX].astype(jnp.float32)
    imag = slot_ref[:, PIX:].astype(jnp.float32)
    table = lax.dot_general(
        real * real + imag * imag, power, NT, precision=HIGH, preferred_element_type=jnp.float32
    )
    table = -0.5 * table + prior
    first = table.astype(jnp.bfloat16).astype(jnp.float32)
    rest = table - first
    second = rest.astype(jnp.bfloat16).astype(jnp.float32)
    third = rest - second
    chunks(1, jnp.concatenate([first, second, third, jnp.zeros_like(first)], axis=1))


def panel(owners, priors, slots, contrast, noise):
    return pl.pallas_call(
        panel_kernel,
        out_shape=jax.ShapeDtypeStruct((NDP * 8, QUART), jnp.bfloat16),
        in_specs=[anywhere()] * 5,
        out_specs=vmem(),
        scratch_shapes=[
            pltpu.SMEM((CLS,), jnp.int32),
            pltpu.SMEM((CLS,), jnp.float32),
            pltpu.VMEM((ROWS, FEAT), jnp.bfloat16),
            pltpu.VMEM((GRP, PIX), jnp.float32),
            pltpu.VMEM((PIX,), jnp.float32),
            pltpu.SemaphoreType.DMA((5,)),
        ],
        compiler_params=params(60),
        name="panel",
    )(owners, priors, slots, contrast, noise)


def pick_kernel(owners_ref, got_ref, out_ref, sems):
    copies = [
        pltpu.make_async_copy(got_ref.at[owners_ref[k]], out_ref.at[k], sems.at[k])
        for k in range(CLS)
    ]
    for copy in copies:
        copy.start()
    for copy in copies:
        copy.wait()


def pick(owners, got):
    return pl.pallas_call(
        pick_kernel,
        out_shape=jax.ShapeDtypeStruct((CLS, 8, QUART), jnp.bfloat16),
        in_specs=[smem(), anywhere()],
        out_specs=vmem(),
        scratch_shapes=[pltpu.SemaphoreType.DMA((CLS,))],
        compiler_params=params(16),
        name="pick",
    )(owners, got)


def settle_kernel(in_ref, out_ref, sem):
    copy = pltpu.make_async_copy(in_ref, out_ref, sem)
    copy.start()
    copy.wait()


def settle(array):
    return pl.pallas_call(
        settle_kernel,
        out_shape=jax.ShapeDtypeStruct(array.shape, array.dtype),
        in_specs=[anywhere()],
        out_specs=vmem(),
        scratch_shapes=[pltpu.SemaphoreType.DMA],
        compiler_params=params(16),
        name="settle",
    )(array)


def scores_kernel(owners, plan, *refs):
    n_panels = sum(count for _, count, _ in plan)
    panels, images, outs = refs[:n_panels], refs[n_panels : n_panels + NOR], refs[n_panels + NOR :]
    at = 0
    for chain, count, first in plan:
        panel = jnp.concatenate([ref[...] for ref in panels[at : at + count]], axis=0)
        for owner, out in zip(owners, outs):
            image = jnp.concatenate([ref[owner, chain] for ref in images], axis=0)
            part = lax.dot_general(panel, image, NT, preferred_element_type=jnp.float32)
            if at == 0:
                out[...] = part
            else:
                out[first : first + panel.shape[0]] += part
        at += count


def scores_of(panels, images, owners, plan):
    rows = plan[0][1] * CLS * 8
    outs = len(owners)
    return pl.pallas_call(
        functools.partial(scores_kernel, owners, plan),
        out_shape=[jax.ShapeDtypeStruct((rows, GROUP_ROWS), jnp.float32)] * outs,
        in_specs=[vmem()] * (len(panels) + NOR),
        out_specs=[vmem()] * outs,
        compiler_params=params(16),
        cost_estimate=pl.CostEstimate(
            flops=8 * len(panels) * CLS * 8 * GROUP_ROWS * QUART * outs,
            bytes_accessed=8 * MIB,
            transcendentals=0,
        ),
        name="scores",
    )(*panels, *images)


def swap_halves(lanes, yhi):
    pieces = [
        pltpu.roll(lanes[:, k : k + 2 * ROWS], yhi * ROWS, 1)
        for k in range(0, GROUP_ROWS, 2 * ROWS)
    ]
    return jnp.concatenate(pieces, axis=1)


def norms_kernel(near_ref, near_other_ref, far_ref, far_other_ref, scores_ref, parts_ref):
    _, _, _, x, yhi = place()
    near = near_ref[...] + near_other_ref[...]
    far = far_ref[...] + far_other_ref[...]
    step = CLS * 8
    rows = [near[k : k + step] for k in range(0, NZ * step, step)]
    for k in range(3):
        rows[5 + k] += far[k * step : (k + 1) * step]
    scores = jnp.concatenate([rows[k] for k in (0, 1, 2, 5, 7, 6, 3, 4)], axis=0)
    scores_ref[...] = scores
    scores = scores.reshape(NZ, CLS, 8, GROUP_ROWS)
    maximum = jnp.max(jnp.max(scores, axis=0), axis=1, keepdims=True)
    totals = jnp.sum(jnp.sum(jnp.exp(scores - maximum[None]), axis=0), axis=1)
    lse = swap_halves(maximum[:, 0, :] + jnp.log(totals), yhi)
    lse = pltpu.roll(lse, x * 2 * ROWS, 1)
    parts_ref[...] = jnp.broadcast_to(lse[None], parts_ref.shape)


def norms(*scores):
    return pl.pallas_call(
        norms_kernel,
        out_shape=(
            jax.ShapeDtypeStruct((NZ * CLS * 8, GROUP_ROWS), jnp.float32),
            jax.ShapeDtypeStruct((NOR, CLS, GROUP_ROWS), jnp.float32),
        ),
        in_specs=[vmem()] * 4,
        out_specs=(vmem(), vmem()),
        compiler_params=params(24),
        name="norms",
    )(*scores)


def finish_kernel(parts_ref, scores_ref, evidence_ref, posterior_ref, mass_ref):
    z, _, _, x, yhi = place()
    parts = parts_ref[...]
    maximum = jnp.max(parts, axis=0)
    class_lse = maximum + jnp.log(jnp.sum(jnp.exp(parts - maximum[None]), axis=0))
    top = jnp.max(class_lse, axis=0, keepdims=True)
    evidence = top + jnp.log(jnp.sum(jnp.exp(class_lse - top), axis=0, keepdims=True))
    evidence_ref[...] = evidence
    posterior_ref[...] = jnp.exp(class_lse - evidence)
    here = swap_halves(pltpu.roll(evidence, ((NX - x) % NX) * 2 * ROWS, 1), yhi)
    terms = jnp.exp(scores_ref[...] - here)
    ones = jnp.ones((8, GROUP_ROWS), jnp.float32)
    mass = lax.dot_general(ones, terms, NT, precision=HIGH, preferred_element_type=jnp.float32)
    mass = pltpu.roll(mass, z * CLS * 8, 1)[:1]
    for k in range(NDP):
        mass_ref[k] = mass


def finish(parts, scores):
    return pl.pallas_call(
        finish_kernel,
        out_shape=(
            jax.ShapeDtypeStruct((1, GROUP_ROWS), jnp.float32),
            jax.ShapeDtypeStruct((CLS, GROUP_ROWS), jnp.float32),
            jax.ShapeDtypeStruct((NDP, 1, NZ * CLS * 8), jnp.float32),
        ),
        in_specs=[vmem(), vmem()],
        out_specs=(vmem(), vmem(), vmem()),
        compiler_params=params(24),
        name="finish",
    )(parts, scores)


def together(*arrays):
    return lax.optimization_barrier(arrays)


def per_device(images, groups, panel_slots, owners, contrast, noise_weight, class_prior):
    orient = lax.axis_index("orient")
    noise = noise_weight.reshape(1, PIX)

    sent = panel(owners, class_prior, panel_slots, contrast, noise_weight).reshape(NDP, 8, QUART)
    sent, images = together(sent, images)
    got = lax.all_to_all(sent, "dp", 0, 0)

    weighted = weigh(images, groups.reshape(ROWS, 1), contrast, noise)
    own = jnp.stack([weighted[0], other_core(weighted[1])])
    across, left, right = other_yhi(own), from_left(own), from_right(own)

    got, left, right = together(got, left, right)
    half = CLS * 4
    mine0 = pick(owners, got).reshape(CLS * 8, QUART)
    mine1, mine7 = from_above(mine0), from_below(mine0)
    theirs0 = other_ylo(mine0)
    turn, _ = together(jnp.where(lax.axis_index("dp") % 2 == 0, left, right), mine0)
    far = both_ways_along_x(turn)
    mine1, mine7, across = together(mine1, mine7, across)
    mine2, mine6 = from_above(mine1), from_below(mine7)
    mine2, mine6, theirs0, across, far = together(mine2, mine6, theirs0, across, far)
    pair3 = from_above(jnp.stack([mine2, theirs0]))
    pair5 = from_below(jnp.stack([mine6, theirs0]))
    left_across, right_across, far_across = from_left(across), from_right(across), other_yhi(far)
    pair3, pair5 = together(pair3, pair5)
    mine3, theirs1 = pair3
    mine5, theirs7 = pair5
    next4 = from_above(jnp.concatenate([mine3[half:], theirs1], axis=0))
    next6 = from_below(jnp.concatenate([mine5[:half], theirs7], axis=0))
    next4, next6 = together(next4, next6)
    theirs2, theirs6 = next4[half:], next6[half:]
    mine4 = jnp.concatenate([next6[:half], next4[:half]], axis=0)
    theirs4 = other_ylo(mine4)
    theirs3, theirs5 = from_above(theirs2), from_below(theirs6)
    across = settle(across)
    whole = [own, across, right, right_across, far, far_across, left, left_across]
    near = [mine0, mine1, mine2, mine6, mine7, mine3, mine5, mine4]
    near += [theirs0, theirs1, theirs2, theirs6, theirs7]
    near_plan = ((0, 8, 0), (1, 5, 0))
    (near_theirs,) = scores_of(near, whole, (1,), near_plan)
    near_other = other_core(near_theirs)
    (near_mine,) = scores_of(near, whole, (0,), near_plan)
    near_mine, theirs4 = together(near_mine, theirs4)
    far_panels, far_plan = [theirs3, theirs5, theirs4], ((1, 3, 0),)
    (far_theirs,) = scores_of(far_panels, whole, (1,), far_plan)
    far_other = other_core(far_theirs)
    (far_mine,) = scores_of(far_panels, whole, (0,), far_plan)
    scores, partial = norms(near_mine, near_other, far_mine, far_other)
    parts = lax.all_to_all(partial, "orient", 0, 0)
    evidence, posterior, mass = finish(parts, scores)
    masses = lax.all_to_all(mass, "dp", 0, 0)
    normalise = CLS * ORI * NOR / (ROWS * NOR * NDP)
    total = jnp.sum(masses, axis=(0, 1)) * normalise
    orientation_mass = total.reshape(NZ, CLS, 8).transpose(1, 0, 2).reshape(CLS, ORI)
    log_evidence = lax.dynamic_slice_in_dim(evidence[0], orient * ROWS, ROWS, 0)
    class_posterior = lax.dynamic_slice_in_dim(posterior, orient * ROWS, ROWS, 1)
    return (log_evidence, class_posterior, orientation_mass)


def solution(mesh):
    return jax.shard_map(
        per_device,
        mesh=mesh,
        in_specs=(
            P(("dp", "orient"), None),
            P(("dp", "orient")),
            P("dp", "orient", None),
            P(),
            P(),
            P(),
            P(),
        ),
        out_specs=(P(("dp", "orient")), P(None, ("dp", "orient")), P(None, "orient")),
        check_vma=False,
    )
```

```python
import functools
import jax
import jax.numpy as jnp
from jax import lax
from jax.experimental import pallas as pl
from jax.experimental.pallas import tpu as pltpu
from jax.sharding import PartitionSpec as P

NX, NZ = 4, 8
NDP, NOR = 32, 8
CLS, PIX, GRP, ORI, ROWS = 8, 4224, 64, 64, 64
FEAT = 2 * PIX
EXT = 256
COLS = FEAT + EXT
HALF = COLS // 2
QUART = COLS // 4
GROUP_ROWS = NOR * ROWS
HIGH = lax.Precision.HIGHEST
NT = (((1,), (1,)), ((), ()))
MIB = 1024 * 1024


def permute(array, move):
    pairs = []
    for dp in range(NDP):
        for orient in range(NOR):
            place = (dp // 4, (dp // 2) % 2, dp % 2, orient // 2, orient % 2)
            z, ylo, core, x, yhi = move(*place)
            target = ((z % NZ) * 4 + ylo * 2 + core) * NOR + (x % NX) * 2 + yhi
            pairs.append((dp * NOR + orient, target))
    return lax.ppermute(array, ("dp", "orient"), pairs)


def other_core(array):
    return permute(array, lambda z, ylo, core, x, yhi: (z, ylo, 1 - core, x, yhi))


def other_ylo(array):
    return permute(array, lambda z, ylo, core, x, yhi: (z, 1 - ylo, core, x, yhi))


def other_yhi(array):
    return permute(array, lambda z, ylo, core, x, yhi: (z, ylo, core, x, 1 - yhi))


def from_below(array):
    return permute(array, lambda z, ylo, core, x, yhi: (z + 1, ylo, core, x, yhi))


def from_above(array):
    return permute(array, lambda z, ylo, core, x, yhi: (z - 1, ylo, core, x, yhi))


def both_ways_along_x(array):
    return permute(
        array, lambda z, ylo, core, x, yhi: (z, ylo, core, x + 1 - 2 * core, yhi)
    )


def from_left(array):
    return permute(array, lambda z, ylo, core, x, yhi: (z, ylo, core, x + 1, yhi))


def from_right(array):
    return permute(array, lambda z, ylo, core, x, yhi: (z, ylo, core, x - 1, yhi))


def vmem():
    return pl.BlockSpec(memory_space=pltpu.VMEM)


def anywhere():
    return pl.BlockSpec(memory_space=pl.ANY)


def smem():
    return pl.BlockSpec(memory_space=pltpu.SMEM)


def params(mib, **more):
    return pltpu.CompilerParams(vmem_limit_bytes=mib * MIB, **more)


def place():
    dp, orient = lax.axis_index("dp"), lax.axis_index("orient")
    return dp // 4, (dp // 2) % 2, dp % 2, orient // 2, orient % 2


def weigh_kernel(images_ref, groups_ref, contrast_ref, noise_ref, out_ref):
    _, ylo, core, _, _ = place()
    hot = (
        groups_ref[...] == lax.broadcasted_iota(jnp.int32, (ROWS, GRP), 1)
    ).astype(jnp.float32)
    rows = jnp.dot(hot, contrast_ref[...], precision=HIGH, preferred_element_type=jnp.float32)
    factor = rows * noise_ref[...]
    real = (images_ref[:, :PIX].astype(jnp.float32) * factor).astype(jnp.bfloat16)
    imag = (images_ref[:, PIX:].astype(jnp.float32) * factor).astype(jnp.bfloat16)
    ext = jnp.concatenate([hot, hot, hot, jnp.zeros_like(hot)], axis=1).astype(jnp.bfloat16)
    out_ref[core, ylo] = real[:, :QUART]
    out_ref[core, 1 - ylo] = jnp.concatenate([real[:, QUART:], imag[:, : HALF - PIX]], axis=1)
    out_ref[1 - core, ylo] = imag[:, HALF - PIX : 3 * QUART - PIX]
    out_ref[1 - core, 1 - ylo] = jnp.concatenate([imag[:, 3 * QUART - PIX :], ext], axis=1)


def weigh(images, groups, contrast, noise):
    return pl.pallas_call(
        weigh_kernel,
        out_shape=jax.ShapeDtypeStruct((2, 2, ROWS, QUART), jnp.bfloat16),
        in_specs=[vmem(), vmem(), vmem(), vmem()],
        out_specs=vmem(),
        compiler_params=params(24),
        name="weigh",
    )(images, groups, contrast, noise)


def panel_kernel(
    owners_hbm, priors_hbm, slot_hbm, contrast_hbm, noise_hbm, out_hbm,
    owners_ref, priors_ref, slot_ref, contrast_ref, noise_ref, out_ref, sems,
):
    pairs = [
        (slot_hbm.at[0], slot_ref),
        (contrast_hbm, contrast_ref),
        (noise_hbm, noise_ref),
        (owners_hbm, owners_ref),
        (priors_hbm, priors_ref),
    ]
    copies = [pltpu.make_async_copy(a, b, sems.at[k]) for k, (a, b) in enumerate(pairs)]
    for copy in copies:
        copy.start()

    def chunks(ylo, ext):
        for z in range(NZ):
            rows = slice(8 * z, 8 * z + 8)
            parts = []
            for core in range(2):
                start = core * HALF + ylo * QUART
                stop = min(start + QUART, FEAT)
                part = slot_ref[:, start:stop].astype(jnp.float32)[rows]
                if stop < start + QUART:
                    part = jnp.concatenate([part, ext[rows]], axis=1)
                parts.append(part)
            out_ref[ylo, z] = jnp.concatenate(parts, axis=0).astype(jnp.bfloat16)
        target = out_hbm.at[:, 16 * ylo : 16 * ylo + 16]
        copy = pltpu.make_async_copy(out_ref.at[ylo], target, sems.at[5 + ylo])
        copy.start()
        return copy

    copies[0].wait()
    out0 = chunks(0, None)
    for copy in copies[1:]:
        copy.wait()
    dp = lax.axis_index("dp")
    prior = jnp.float32(0)
    for k in range(CLS):
        prior += jnp.where(owners_ref[k] == dp, priors_ref[k], jnp.float32(0))
    contrast = contrast_ref[...]
    power = contrast * contrast * noise_ref[...].reshape(1, PIX)
    real = slot_ref[:, :PIX].astype(jnp.float32)
    imag = slot_ref[:, PIX:].astype(jnp.float32)
    table = lax.dot_general(
        real * real + imag * imag, power, NT, precision=HIGH, preferred_element_type=jnp.float32
    )
    table = -0.5 * table + prior
    first = table.astype(jnp.bfloat16).astype(jnp.float32)
    rest = table - first
    second = rest.astype(jnp.bfloat16).astype(jnp.float32)
    third = rest - second
    out1 = chunks(1, jnp.concatenate([first, second, third, jnp.zeros_like(first)], axis=1))
    out0.wait()
    out1.wait()


def panel(owners, priors, slots, contrast, noise):
    return pl.pallas_call(
        panel_kernel,
        out_shape=jax.ShapeDtypeStruct((NZ, 32, QUART), jnp.bfloat16),
        in_specs=[anywhere()] * 5,
        out_specs=anywhere(),
        scratch_shapes=[
            pltpu.SMEM((CLS,), jnp.int32),
            pltpu.SMEM((CLS,), jnp.float32),
            pltpu.VMEM((ROWS, FEAT), jnp.bfloat16),
            pltpu.VMEM((GRP, PIX), jnp.float32),
            pltpu.VMEM((PIX,), jnp.float32),
            pltpu.VMEM((2, NZ, 16, QUART), jnp.bfloat16),
            pltpu.SemaphoreType.DMA((7,)),
        ],
        compiler_params=params(60),
        name="panel",
    )(owners, priors, slots, contrast, noise)


def pick_kernel(owners_ref, got_ref, out_ref, sems):
    copies = [
        pltpu.make_async_copy(got_ref.at[owners_ref[k]], out_ref.at[k], sems.at[k])
        for k in range(CLS)
    ]
    for copy in copies:
        copy.start()
    for copy in copies:
        copy.wait()


def pick(owners, got):
    return pl.pallas_call(
        pick_kernel,
        out_shape=jax.ShapeDtypeStruct((CLS, 8, QUART), jnp.bfloat16),
        in_specs=[smem(), anywhere()],
        out_specs=vmem(),
        scratch_shapes=[pltpu.SemaphoreType.DMA((CLS,))],
        compiler_params=params(16),
        name="pick",
    )(owners, got)


def settle_kernel(in_ref, out_ref, sem):
    copy = pltpu.make_async_copy(in_ref, out_ref, sem)
    copy.start()
    copy.wait()


def settle(array):
    return pl.pallas_call(
        settle_kernel,
        out_shape=jax.ShapeDtypeStruct(array.shape, array.dtype),
        in_specs=[anywhere()],
        out_specs=vmem(),
        scratch_shapes=[pltpu.SemaphoreType.DMA],
        compiler_params=params(16),
        name="settle",
    )(array)


def scores_kernel(owners, plan, *refs):
    n_panels = sum(count for _, count, _ in plan)
    panels, images, outs = refs[:n_panels], refs[n_panels : n_panels + NOR], refs[n_panels + NOR :]
    at = 0
    for chain, count, first in plan:
        panel = jnp.concatenate([ref[...] for ref in panels[at : at + count]], axis=0)
        for owner, out in zip(owners, outs):
            image = jnp.concatenate([ref[owner, chain] for ref in images], axis=0)
            part = lax.dot_general(panel, image, NT, preferred_element_type=jnp.float32)
            if at == 0:
                out[...] = part
            else:
                out[first : first + panel.shape[0]] += part
        at += count


def scores_of(panels, images, owners, plan):
    rows = plan[0][1] * CLS * 8
    outs = len(owners)
    return pl.pallas_call(
        functools.partial(scores_kernel, owners, plan),
        out_shape=[jax.ShapeDtypeStruct((rows, GROUP_ROWS), jnp.float32)] * outs,
        in_specs=[vmem()] * (len(panels) + NOR),
        out_specs=[vmem()] * outs,
        compiler_params=params(16),
        cost_estimate=pl.CostEstimate(
            flops=8 * len(panels) * CLS * 8 * GROUP_ROWS * QUART * outs,
            bytes_accessed=8 * MIB,
            transcendentals=0,
        ),
        name="scores",
    )(*panels, *images)


def swap_halves(lanes, yhi):
    pieces = [
        pltpu.roll(lanes[:, k : k + 2 * ROWS], yhi * ROWS, 1)
        for k in range(0, GROUP_ROWS, 2 * ROWS)
    ]
    return jnp.concatenate(pieces, axis=1)


def norms_kernel(near_ref, near_other_ref, far_ref, far_other_ref, scores_ref, parts_ref):
    z, _, _, x, yhi = place()
    near = near_ref[...] + near_other_ref[...]
    far = far_ref[...] + far_other_ref[...]
    step = CLS * 8
    rows = [near[k : k + step] for k in range(0, NZ * step, step)]
    for k in range(3):
        rows[5 + k] += far[k * step : (k + 1) * step]
    rows = [rows[k].reshape(CLS, 8, GROUP_ROWS) for k in (0, 1, 2, 5, 7, 6, 3, 4)]
    for k in range(NZ):
        at = pl.multiple_of(((z + k) % NZ) * 8, 8)
        for c in range(CLS):
            scores_ref[c, pl.ds(at, 8), :] = rows[k][c]
    maximum = functools.reduce(jnp.maximum, rows)
    maximum = jnp.max(maximum, axis=1, keepdims=True)
    totals = sum(jnp.exp(part - maximum) for part in rows)
    totals = jnp.sum(totals, axis=1)
    lse = swap_halves(maximum[:, 0, :] + jnp.log(totals), yhi)
    lse = pltpu.roll(lse, x * 2 * ROWS, 1)
    parts_ref[...] = jnp.broadcast_to(lse[None], parts_ref.shape)


def norms(*scores):
    return pl.pallas_call(
        norms_kernel,
        out_shape=(
            jax.ShapeDtypeStruct((CLS, ORI, GROUP_ROWS), jnp.float32),
            jax.ShapeDtypeStruct((NOR, CLS, GROUP_ROWS), jnp.float32),
        ),
        in_specs=[vmem()] * 4,
        out_specs=(vmem(), vmem()),
        compiler_params=params(24),
        name="norms",
    )(*scores)


def finish_kernel(parts_ref, scores_ref, evidence_ref, posterior_ref, mass_ref):
    _, _, _, x, yhi = place()
    parts = parts_ref[...]
    maximum = jnp.max(parts, axis=0)
    class_lse = maximum + jnp.log(jnp.sum(jnp.exp(parts - maximum[None]), axis=0))
    top = jnp.max(class_lse, axis=0, keepdims=True)
    evidence = top + jnp.log(jnp.sum(jnp.exp(class_lse - top), axis=0, keepdims=True))
    evidence_ref[...] = evidence
    posterior_ref[...] = jnp.exp(class_lse - evidence)
    here = swap_halves(pltpu.roll(evidence, ((NX - x) % NX) * 2 * ROWS, 1), yhi)
    terms = jnp.exp(scores_ref[...].reshape(CLS * ORI, GROUP_ROWS) - here)
    ones = jnp.ones((8, GROUP_ROWS), jnp.bfloat16)
    mass = jnp.zeros((8, terms.shape[0]), jnp.float32)
    for _ in range(3):
        piece = terms.astype(jnp.bfloat16)
        mass += lax.dot_general(ones, piece, NT, preferred_element_type=jnp.float32)
        terms = terms - piece.astype(jnp.float32)
    mass = mass[:1] * (CLS * ORI * NOR / (ROWS * NOR * NDP))
    for k in range(NDP):
        mass_ref[k] = mass


def finish(parts, scores):
    return pl.pallas_call(
        finish_kernel,
        out_shape=(
            jax.ShapeDtypeStruct((1, GROUP_ROWS), jnp.float32),
            jax.ShapeDtypeStruct((CLS, GROUP_ROWS), jnp.float32),
            jax.ShapeDtypeStruct((NDP, 1, CLS * ORI), jnp.float32),
        ),
        in_specs=[vmem(), vmem()],
        out_specs=(vmem(), vmem(), vmem()),
        compiler_params=params(24),
        name="finish",
    )(parts, scores)


def together(*arrays):
    return lax.optimization_barrier(arrays)


def per_device(images, groups, panel_slots, owners, contrast, noise_weight, class_prior):
    orient = lax.axis_index("orient")
    noise = noise_weight.reshape(1, PIX)

    sent = panel(owners, class_prior, panel_slots, contrast, noise_weight).reshape(NDP, 8, QUART)
    sent, images = together(sent, images)
    got = lax.all_to_all(sent, "dp", 0, 0)

    weighted = weigh(images, groups.reshape(ROWS, 1), contrast, noise)
    own = jnp.stack([weighted[0], other_core(weighted[1])])
    across, left, right = other_yhi(own), from_left(own), from_right(own)

    got, left, right = together(got, left, right)
    half = CLS * 4
    mine0 = pick(owners, got).reshape(CLS * 8, QUART)
    mine1, mine7 = from_above(mine0), from_below(mine0)
    theirs0 = other_ylo(mine0)
    turn = jnp.where(lax.axis_index("dp") % 2 == 0, left, right)
    far = both_ways_along_x(turn)
    mine1, mine7, across = together(mine1, mine7, across)
    mine2, mine6 = from_above(mine1), from_below(mine7)
    mine2, mine6, theirs0, across, far = together(mine2, mine6, theirs0, across, far)
    pair3 = from_above(jnp.stack([mine2, theirs0]))
    pair5 = from_below(jnp.stack([mine6, theirs0]))
    left_across, right_across, far_across = from_left(across), from_right(across), other_yhi(far)
    pair3, pair5 = together(pair3, pair5)
    mine3, theirs1 = pair3
    mine5, theirs7 = pair5
    next4 = from_above(jnp.concatenate([mine3[half:], theirs1], axis=0))
    next6 = from_below(jnp.concatenate([mine5[:half], theirs7], axis=0))
    next4, next6 = together(next4, next6)
    theirs2, theirs6 = next4[half:], next6[half:]
    mine4 = jnp.concatenate([next6[:half], next4[:half]], axis=0)
    theirs4 = other_ylo(mine4)
    theirs3, theirs5 = from_above(theirs2), from_below(theirs6)
    across = settle(across)
    whole = [own, across, right, right_across, far, far_across, left, left_across]
    near = [mine0, mine1, mine2, mine6, mine7, mine3, mine5, mine4]
    near += [theirs0, theirs1, theirs2, theirs6, theirs7]
    near_plan = ((0, 8, 0), (1, 5, 0))
    (near_theirs,) = scores_of(near, whole, (1,), near_plan)
    near_other = other_core(near_theirs)
    (near_mine,) = scores_of(near, whole, (0,), near_plan)
    near_mine, theirs4 = together(near_mine, theirs4)
    far_panels, far_plan = [theirs3, theirs5, theirs4], ((1, 3, 0),)
    (far_theirs,) = scores_of(far_panels, whole, (1,), far_plan)
    far_other = other_core(far_theirs)
    (far_mine,) = scores_of(far_panels, whole, (0,), far_plan)
    scores, partial = norms(near_mine, near_other, far_mine, far_other)
    parts = lax.all_to_all(partial, "orient", 0, 0)
    evidence, posterior, mass = finish(parts, scores)
    masses = lax.all_to_all(mass, "dp", 0, 0)
    orientation_mass = jnp.sum(masses, axis=(0, 1)).reshape(CLS, ORI)
    log_evidence = lax.dynamic_slice_in_dim(evidence[0], orient * ROWS, ROWS, 0)
    class_posterior = lax.dynamic_slice_in_dim(posterior, orient * ROWS, ROWS, 1)
    return (log_evidence, class_posterior, orientation_mass)


def solution(mesh):
    return jax.shard_map(
        per_device,
        mesh=mesh,
        in_specs=(
            P(("dp", "orient"), None),
            P(("dp", "orient")),
            P("dp", "orient", None),
            P(),
            P(),
            P(),
            P(),
        ),
        out_specs=(P(("dp", "orient")), P(None, ("dp", "orient")), P(None, "orient")),
        check_vma=False,
    )
```

```python
import functools
import jax
import jax.numpy as jnp
from jax import lax
from jax.experimental import pallas as pl
from jax.experimental.pallas import tpu as pltpu
from jax.sharding import PartitionSpec as P

NX, NZ = 4, 8
NDP, NOR = 32, 8
CLS, PIX, GRP, ORI, ROWS = 8, 4224, 64, 64, 64
FEAT = 2 * PIX
EXT = 256
COLS = FEAT + EXT
HALF = COLS // 2
QUART = COLS // 4
GROUP_ROWS = NOR * ROWS
HIGH = lax.Precision.HIGHEST
NT = (((1,), (1,)), ((), ()))
MIB = 1024 * 1024


def permute(array, move):
    pairs = []
    for dp in range(NDP):
        for orient in range(NOR):
            place = (dp // 4, (dp // 2) % 2, dp % 2, orient // 2, orient % 2)
            z, ylo, core, x, yhi = move(*place)
            target = ((z % NZ) * 4 + ylo * 2 + core) * NOR + (x % NX) * 2 + yhi
            pairs.append((dp * NOR + orient, target))
    return lax.ppermute(array, ("dp", "orient"), pairs)


def other_core(array):
    return permute(array, lambda z, ylo, core, x, yhi: (z, ylo, 1 - core, x, yhi))


def other_ylo(array):
    return permute(array, lambda z, ylo, core, x, yhi: (z, 1 - ylo, core, x, yhi))


def other_yhi(array):
    return permute(array, lambda z, ylo, core, x, yhi: (z, ylo, core, x, 1 - yhi))


def from_below(array):
    return permute(array, lambda z, ylo, core, x, yhi: (z + 1, ylo, core, x, yhi))


def from_above(array):
    return permute(array, lambda z, ylo, core, x, yhi: (z - 1, ylo, core, x, yhi))


def both_ways_along_x(array):
    return permute(
        array, lambda z, ylo, core, x, yhi: (z, ylo, core, x + 1 - 2 * core, yhi)
    )


def from_left(array):
    return permute(array, lambda z, ylo, core, x, yhi: (z, ylo, core, x + 1, yhi))


def from_right(array):
    return permute(array, lambda z, ylo, core, x, yhi: (z, ylo, core, x - 1, yhi))


def vmem():
    return pl.BlockSpec(memory_space=pltpu.VMEM)


def anywhere():
    return pl.BlockSpec(memory_space=pl.ANY)


def smem():
    return pl.BlockSpec(memory_space=pltpu.SMEM)


def params(mib, **more):
    return pltpu.CompilerParams(vmem_limit_bytes=mib * MIB, **more)


def place():
    dp, orient = lax.axis_index("dp"), lax.axis_index("orient")
    return dp // 4, (dp // 2) % 2, dp % 2, orient // 2, orient % 2


def weigh_kernel(images_ref, groups_ref, contrast_ref, noise_ref, out_ref):
    _, ylo, core, _, _ = place()
    hot = (
        groups_ref[...] == lax.broadcasted_iota(jnp.int32, (ROWS, GRP), 1)
    ).astype(jnp.float32)
    rows = jnp.dot(hot, contrast_ref[...], precision=HIGH, preferred_element_type=jnp.float32)
    factor = rows * noise_ref[...]
    real = (images_ref[:, :PIX].astype(jnp.float32) * factor).astype(jnp.bfloat16)
    imag = (images_ref[:, PIX:].astype(jnp.float32) * factor).astype(jnp.bfloat16)
    ext = jnp.concatenate([hot, hot, hot, jnp.zeros_like(hot)], axis=1).astype(jnp.bfloat16)
    out_ref[core, ylo] = real[:, :QUART]
    out_ref[core, 1 - ylo] = jnp.concatenate([real[:, QUART:], imag[:, : HALF - PIX]], axis=1)
    out_ref[1 - core, ylo] = imag[:, HALF - PIX : 3 * QUART - PIX]
    out_ref[1 - core, 1 - ylo] = jnp.concatenate([imag[:, 3 * QUART - PIX :], ext], axis=1)


def weigh(images, groups, contrast, noise):
    return pl.pallas_call(
        weigh_kernel,
        out_shape=jax.ShapeDtypeStruct((2, 2, ROWS, QUART), jnp.bfloat16),
        in_specs=[vmem(), vmem(), vmem(), vmem()],
        out_specs=vmem(),
        compiler_params=params(24),
        name="weigh",
    )(images, groups, contrast, noise)


def panel_kernel(
    owners_hbm, priors_hbm, slot_hbm, contrast_hbm, noise_hbm, out_hbm,
    owners_ref, priors_ref, slot_ref, contrast_ref, noise_ref, out_ref, sems,
):
    pairs = [
        (slot_hbm.at[0], slot_ref),
        (contrast_hbm, contrast_ref),
        (noise_hbm, noise_ref),
        (owners_hbm, owners_ref),
        (priors_hbm, priors_ref),
    ]
    copies = [pltpu.make_async_copy(a, b, sems.at[k]) for k, (a, b) in enumerate(pairs)]
    for copy in copies:
        copy.start()

    def chunks(ylo, ext):
        for z in range(NZ):
            rows = slice(8 * z, 8 * z + 8)
            parts = []
            for core in range(2):
                start = core * HALF + ylo * QUART
                stop = min(start + QUART, FEAT)
                part = slot_ref[:, start:stop].astype(jnp.float32)[rows]
                if stop < start + QUART:
                    part = jnp.concatenate([part, ext[rows]], axis=1)
                parts.append(part)
            out_ref[ylo, z] = jnp.concatenate(parts, axis=0).astype(jnp.bfloat16)
        target = out_hbm.at[:, 16 * ylo : 16 * ylo + 16]
        copy = pltpu.make_async_copy(out_ref.at[ylo], target, sems.at[5 + ylo])
        copy.start()
        return copy

    copies[0].wait()
    out0 = chunks(0, None)
    for copy in copies[1:]:
        copy.wait()
    dp = lax.axis_index("dp")
    prior = jnp.float32(0)
    for k in range(CLS):
        prior += jnp.where(owners_ref[k] == dp, priors_ref[k], jnp.float32(0))
    contrast = contrast_ref[...]
    power = contrast * contrast * noise_ref[...].reshape(1, PIX)
    real = slot_ref[:, :PIX].astype(jnp.float32)
    imag = slot_ref[:, PIX:].astype(jnp.float32)
    table = lax.dot_general(
        real * real + imag * imag, power, NT, precision=HIGH, preferred_element_type=jnp.float32
    )
    table = -0.5 * table + prior
    first = table.astype(jnp.bfloat16).astype(jnp.float32)
    rest = table - first
    second = rest.astype(jnp.bfloat16).astype(jnp.float32)
    third = rest - second
    out1 = chunks(1, jnp.concatenate([first, second, third, jnp.zeros_like(first)], axis=1))
    out0.wait()
    out1.wait()


def panel(owners, priors, slots, contrast, noise):
    return pl.pallas_call(
        panel_kernel,
        out_shape=jax.ShapeDtypeStruct((NZ, 32, QUART), jnp.bfloat16),
        in_specs=[anywhere()] * 5,
        out_specs=anywhere(),
        scratch_shapes=[
            pltpu.SMEM((CLS,), jnp.int32),
            pltpu.SMEM((CLS,), jnp.float32),
            pltpu.VMEM((ROWS, FEAT), jnp.bfloat16),
            pltpu.VMEM((GRP, PIX), jnp.float32),
            pltpu.VMEM((PIX,), jnp.float32),
            pltpu.VMEM((2, NZ, 16, QUART), jnp.bfloat16),
            pltpu.SemaphoreType.DMA((7,)),
        ],
        compiler_params=params(60),
        name="panel",
    )(owners, priors, slots, contrast, noise)


def pick_kernel(owners_ref, got_ref, out_ref, sems):
    copies = [
        pltpu.make_async_copy(got_ref.at[owners_ref[k]], out_ref.at[k], sems.at[k])
        for k in range(CLS)
    ]
    for copy in copies:
        copy.start()
    for copy in copies:
        copy.wait()


def pick(owners, got):
    return pl.pallas_call(
        pick_kernel,
        out_shape=jax.ShapeDtypeStruct((CLS, 8, QUART), jnp.bfloat16),
        in_specs=[smem(), anywhere()],
        out_specs=vmem(),
        scratch_shapes=[pltpu.SemaphoreType.DMA((CLS,))],
        compiler_params=params(16),
        name="pick",
    )(owners, got)


def settle_kernel(in_ref, out_ref, sem):
    copy = pltpu.make_async_copy(in_ref, out_ref, sem)
    copy.start()
    copy.wait()


def settle(array):
    return pl.pallas_call(
        settle_kernel,
        out_shape=jax.ShapeDtypeStruct(array.shape, array.dtype),
        in_specs=[anywhere()],
        out_specs=vmem(),
        scratch_shapes=[pltpu.SemaphoreType.DMA],
        compiler_params=params(16),
        name="settle",
    )(array)


def scores_kernel(owners, plan, *refs):
    n_panels = sum(count for _, count, _ in plan)
    panels, images, outs = refs[:n_panels], refs[n_panels : n_panels + NOR], refs[n_panels + NOR :]
    at = 0
    for chain, count, first in plan:
        panel = jnp.concatenate([ref[...] for ref in panels[at : at + count]], axis=0)
        for owner, out in zip(owners, outs):
            image = jnp.concatenate([ref[owner, chain] for ref in images], axis=0)
            part = lax.dot_general(panel, image, NT, preferred_element_type=jnp.float32)
            if at == 0:
                out[...] = part
            else:
                out[first : first + panel.shape[0]] += part
        at += count


def scores_of(panels, images, owners, plan):
    rows = plan[0][1] * CLS * 8
    outs = len(owners)
    return pl.pallas_call(
        functools.partial(scores_kernel, owners, plan),
        out_shape=[jax.ShapeDtypeStruct((rows, GROUP_ROWS), jnp.float32)] * outs,
        in_specs=[vmem()] * (len(panels) + NOR),
        out_specs=[vmem()] * outs,
        compiler_params=params(16),
        cost_estimate=pl.CostEstimate(
            flops=8 * len(panels) * CLS * 8 * GROUP_ROWS * QUART * outs,
            bytes_accessed=8 * MIB,
            transcendentals=0,
        ),
        name="scores",
    )(*panels, *images)


def swap_halves(lanes, yhi):
    pieces = [
        pltpu.roll(lanes[:, k : k + 2 * ROWS], yhi * ROWS, 1)
        for k in range(0, GROUP_ROWS, 2 * ROWS)
    ]
    return jnp.concatenate(pieces, axis=1)


def norms_kernel(near_ref, near_other_ref, far_ref, far_other_ref, scores_ref, parts_ref):
    z, _, _, x, yhi = place()
    near = near_ref[...] + near_other_ref[...]
    far = far_ref[...] + far_other_ref[...]
    step = CLS * 8
    rows = [near[k : k + step] for k in range(0, NZ * step, step)]
    for k in range(3):
        rows[5 + k] += far[k * step : (k + 1) * step]
    rows = [rows[k].reshape(CLS, 8, GROUP_ROWS) for k in (0, 1, 2, 5, 7, 6, 3, 4)]
    for k in range(NZ):
        at = pl.multiple_of(((z + k) % NZ) * 8, 8)
        for c in range(CLS):
            scores_ref[c, pl.ds(at, 8), :] = rows[k][c]
    maximum = functools.reduce(jnp.maximum, rows)
    maximum = jnp.max(maximum, axis=1, keepdims=True)
    totals = sum(jnp.exp(part - maximum) for part in rows)
    totals = jnp.sum(totals, axis=1)
    lse = swap_halves(maximum[:, 0, :] + jnp.log(totals), yhi)
    lse = pltpu.roll(lse, x * 2 * ROWS, 1)
    parts_ref[...] = jnp.broadcast_to(lse[None], parts_ref.shape)


def norms(*scores):
    return pl.pallas_call(
        norms_kernel,
        out_shape=(
            jax.ShapeDtypeStruct((CLS, ORI, GROUP_ROWS), jnp.float32),
            jax.ShapeDtypeStruct((NOR, CLS, GROUP_ROWS), jnp.float32),
        ),
        in_specs=[vmem()] * 4,
        out_specs=(vmem(), vmem()),
        compiler_params=params(24),
        name="norms",
    )(*scores)


def finish_kernel(parts_ref, scores_ref, evidence_ref, posterior_ref, mass_ref):
    _, _, _, x, yhi = place()
    parts = parts_ref[...]
    maximum = jnp.max(parts, axis=0)
    class_lse = maximum + jnp.log(jnp.sum(jnp.exp(parts - maximum[None]), axis=0))
    top = jnp.max(class_lse, axis=0, keepdims=True)
    evidence = top + jnp.log(jnp.sum(jnp.exp(class_lse - top), axis=0, keepdims=True))
    evidence_ref[...] = evidence
    posterior_ref[...] = jnp.exp(class_lse - evidence)
    here = swap_halves(pltpu.roll(evidence, ((NX - x) % NX) * 2 * ROWS, 1), yhi)
    terms = jnp.exp(scores_ref[...].reshape(CLS * ORI, GROUP_ROWS) - here)
    ones = jnp.ones((8, GROUP_ROWS), jnp.bfloat16)
    mass = jnp.zeros((8, terms.shape[0]), jnp.float32)
    for _ in range(3):
        piece = terms.astype(jnp.bfloat16)
        mass += lax.dot_general(ones, piece, NT, preferred_element_type=jnp.float32)
        terms = terms - piece.astype(jnp.float32)
    mass = mass[:1] * (CLS * ORI * NOR / (ROWS * NOR * NDP))
    for k in range(NDP):
        mass_ref[k] = mass


def finish(parts, scores):
    return pl.pallas_call(
        finish_kernel,
        out_shape=(
            jax.ShapeDtypeStruct((1, GROUP_ROWS), jnp.float32),
            jax.ShapeDtypeStruct((CLS, GROUP_ROWS), jnp.float32),
            jax.ShapeDtypeStruct((NDP, 1, CLS * ORI), jnp.float32),
        ),
        in_specs=[vmem(), vmem()],
        out_specs=(vmem(), vmem(), vmem()),
        compiler_params=params(24),
        name="finish",
    )(parts, scores)


def together(*arrays):
    return lax.optimization_barrier(arrays)


def per_device(images, groups, panel_slots, owners, contrast, noise_weight, class_prior):
    orient = lax.axis_index("orient")
    noise = noise_weight.reshape(1, PIX)

    sent = panel(owners, class_prior, panel_slots, contrast, noise_weight).reshape(NDP, 8, QUART)
    sent, images = together(sent, images)
    got = lax.all_to_all(sent, "dp", 0, 0)

    weighted = weigh(images, groups.reshape(ROWS, 1), contrast, noise)
    own = jnp.stack([weighted[0], other_core(weighted[1])])
    across, left, right = other_yhi(own), from_left(own), from_right(own)

    got, left, right = together(got, left, right)
    half = CLS * 4
    mine0 = pick(owners, got).reshape(CLS * 8, QUART)
    mine1, mine7 = from_above(mine0), from_below(mine0)
    theirs0 = other_ylo(mine0)
    turn = jnp.where(lax.axis_index("dp") % 2 == 0, left, right)
    far = both_ways_along_x(turn)
    mine1, mine7, across = together(mine1, mine7, across)
    mine2, mine6 = from_above(mine1), from_below(mine7)
    mine2, mine6, theirs0, across, far = together(mine2, mine6, theirs0, across, far)
    pair3 = from_above(jnp.stack([mine2, theirs0]))
    pair5 = from_below(jnp.stack([mine6, theirs0]))
    left_across, right_across, far_across = from_left(across), from_right(across), other_yhi(far)
    pair3, pair5 = together(pair3, pair5)
    mine3, theirs1 = pair3
    mine5, theirs7 = pair5
    next4 = from_above(jnp.concatenate([mine3[half:], theirs1], axis=0))
    next6 = from_below(jnp.concatenate([mine5[:half], theirs7], axis=0))
    next4, next6 = together(next4, next6)
    theirs2, theirs6 = next4[half:], next6[half:]
    mine4 = jnp.concatenate([next6[:half], next4[:half]], axis=0)
    theirs4 = other_ylo(mine4)
    theirs3, theirs5 = from_above(theirs2), from_below(theirs6)
    across = settle(across)
    whole = [own, across, right, right_across, far, far_across, left, left_across]
    near = [mine0, mine1, mine2, mine6, mine7, mine3, mine5, mine4]
    near += [theirs0, theirs1, theirs2, theirs6, theirs7]
    near_plan = ((0, 8, 0), (1, 5, 0))
    near_theirs, near_mine = scores_of(near, whole, (1, 0), near_plan)
    near_other = other_core(near_theirs)
    near_mine, theirs4 = together(near_mine, theirs4)
    far_panels, far_plan = [theirs3, theirs5, theirs4], ((1, 3, 0),)
    (far_theirs,) = scores_of(far_panels, whole, (1,), far_plan)
    far_other = other_core(far_theirs)
    (far_mine,) = scores_of(far_panels, whole, (0,), far_plan)
    scores, partial = norms(near_mine, near_other, far_mine, far_other)
    parts = lax.all_to_all(partial, "orient", 0, 0)
    evidence, posterior, mass = finish(parts, scores)
    masses = lax.all_to_all(mass, "dp", 0, 0)
    orientation_mass = jnp.sum(masses, axis=(0, 1)).reshape(CLS, ORI)
    log_evidence = lax.dynamic_slice_in_dim(evidence[0], orient * ROWS, ROWS, 0)
    class_posterior = lax.dynamic_slice_in_dim(posterior, orient * ROWS, ROWS, 1)
    return (log_evidence, class_posterior, orientation_mass)


def solution(mesh):
    return jax.shard_map(
        per_device,
        mesh=mesh,
        in_specs=(
            P(("dp", "orient"), None),
            P(("dp", "orient")),
            P("dp", "orient", None),
            P(),
            P(),
            P(),
            P(),
        ),
        out_specs=(P(("dp", "orient")), P(None, ("dp", "orient")), P(None, "orient")),
        check_vma=False,
    )
```
